512 devices in a mesh: pipe: 128 (over z_lo, y, x, core), seq: 4 (over z_hi).
Axes of the slice: x: 4, y: 8, z: 8 (z_hi: 4, z_lo: 2; z = z_hi * 2 + z_lo), core: 2. Of those that a mesh axis runs over, the one named last changes fastest.
Arguments:
- patches: bfloat16 [128, 512, 1152], P('pipe', 'seq'), may hold values from -3 to 3
- qkv_weight: bfloat16 [128, 1152, 3, 1152], P('pipe', None, None, 'seq'), may hold values from -0.1875 to 0.1875
- out_weight: bfloat16 [128, 1152, 1152], P('pipe', 'seq'), may hold values from -0.1875 to 0.1875
- modulation: float32 [128, 3, 1152], P('pipe'), may hold values from -1.6 to 1.6
- stale_keys: bfloat16 [128, 1024, 1152], P('pipe', None, 'seq'), may hold values from -900 to 900
- stale_values: bfloat16 [128, 1024, 1152], P('pipe', None, 'seq'), may hold values from -6 to 6
- offsets: int32 [128, 2], P('pipe'), may hold values from 0 to 1
Outputs:
- leaving: bfloat16 [128, 512, 1152], P('pipe', 'seq')
The draws below stay inside these ranges and needn't reach their ends.
All inputs are finite; a program needn't handle non-finite values.
Results may differ from the reference program's by a relative error of at most 0.033.
Values may be sent and summed in bfloat16 or wider, within the bound.
No kernel may reach another device: no remote copies, remote signals or barrier semaphores. Data moves between devices by JAX's collectives and lax.ppermute only.
A program may use at most 64 MiB of HBM per device.

```python
import math
import jax
import jax.numpy as jnp
from jax import lax

D = 1152
HEADS = 16
HEAD_DIM = 72
CTX_PATCHES = 2
TICKS = 2
PATCH = 512
CTX = 1024
N_PIPE = 128
N_SEQ = 4


def draw_stale_keys(key, part):
    key = jax.random.fold_in(key, 11)
    base = jax.random.normal(jax.random.fold_in(key, 1), (N_PIPE, CTX, D), jnp.float32)
    return base.astype(jnp.bfloat16)


def place_ends(values, own_key, low, high):
    place = [jax.random.randint(jax.random.fold_in(own_key, axis), (), 0, length) for axis, length in enumerate(values.shape)]
    longest = values.shape.index(max(values.shape))
    next_to = place[:longest] + [(place[longest] + 1) % values.shape[longest]] + place[longest + 1:]
    return values.at[tuple(place)].set(low).at[tuple(next_to)].set(high)


def steps_of(key, shape, pieces, smallest, largest):
    def one(dim, shards_of):
        steps = jax.random.uniform(jax.random.fold_in(jax.random.fold_in(key, 6), dim), (shards_of,), jnp.float32, smallest / len(pieces), largest / len(pieces))
        return jnp.repeat(jnp.exp(steps), shape[dim] // shards_of).reshape((-1,) + (1,) * (len(shape) - dim - 1))

    gain = one(*pieces[0])
    for cut in pieces[1:]:
        gain = gain * one(*cut)
    return gain


def scatter_about(key, shape, scale, most, split=(), dtype=jnp.bfloat16):
    drawn = scale * jax.random.normal(key, shape, jnp.float32)
    if split:
        drawn = drawn * steps_of(key, shape, split, -0.22, 0.18)
    return jnp.clip(drawn, -most, most).astype(dtype)


def setup_inputs(seed: int = 0) -> dict:
    streams_of = jax.random.split(jax.random.key(seed), 8)
    patches = scatter_about(streams_of[0], (N_PIPE, PATCH, D), 0.5, 3.0, ((0, 128), (1, 4)))
    qkv_weight = scatter_about(streams_of[1], (N_PIPE, D, 3, D), D ** -0.5, 0.1875, ((0, 128), (3, 4)))
    out_weight = scatter_about(streams_of[2], (N_PIPE, D, D), D ** -0.5, 0.1875, ((0, 128), (1, 4)))
    modulation = scatter_about(streams_of[3], (N_PIPE, 3, D), 0.4, 1.6, ((0, 128),), jnp.float32)
    stale_keys = draw_stale_keys(jax.random.fold_in(streams_of[7], 71), 0)
    stale_values = scatter_about(streams_of[5], (N_PIPE, CTX, D), 1.0, 6.0, ((0, 128), (2, 4)))
    offsets = place_ends(jax.random.randint(streams_of[6], (N_PIPE, TICKS), 0, CTX_PATCHES), jax.random.fold_in(streams_of[6], 1), 0, CTX_PATCHES - 1).astype(jnp.int32)
    return dict(patches=patches, qkv_weight=qkv_weight, out_weight=out_weight, modulation=modulation, stale_keys=stale_keys, stale_values=stale_values, offsets=offsets)


def normalize(rows, shift, scale):
    values = rows.astype(jnp.float32)
    center = lax.optimization_barrier(jnp.mean(values, axis=-1, keepdims=True))
    spread = lax.optimization_barrier(jnp.mean((values - center) * (values - center), axis=-1, keepdims=True))
    normed = (values - center) * lax.rsqrt(spread + 1e-06)
    return (normed * (1.0 + scale) + shift).astype(jnp.bfloat16)

def layer(hidden, w_qkv, w_out, mods, keys, values, slot):
    count = hidden.shape[0]
    normed = normalize(hidden, mods[0], mods[1])
    qkv = jnp.dot(normed, w_qkv.reshape(D, 3 * D), preferred_element_type=jnp.float32)
    qkv = qkv.astype(jnp.bfloat16).reshape(count, 3, D)
    start = (slot * count).astype(jnp.int32)
    keys = lax.dynamic_update_slice(keys, qkv[:, 1], (start, jnp.int32(0)))
    values = lax.dynamic_update_slice(values, qkv[:, 2], (start, jnp.int32(0)))
    query = qkv[:, 0].reshape(count, HEADS, HEAD_DIM).astype(jnp.float32)
    key_all = keys.reshape(CTX, HEADS, HEAD_DIM).astype(jnp.float32)
    value_all = values.reshape(CTX, HEADS, HEAD_DIM).astype(jnp.float32)
    scores = jnp.einsum('qhd,khd->hqk', query, key_all) * (1.0 / math.sqrt(HEAD_DIM))
    probs = jax.nn.softmax(scores, axis=-1).astype(jnp.bfloat16)
    mixed = jnp.einsum('hqk,khd->qhd', probs.astype(jnp.float32), value_all)
    mixed = mixed.astype(jnp.bfloat16).reshape(count, D)
    width = D // N_SEQ
    partial_value = jnp.einsum('qgc,gcd->gqd', mixed.reshape(count, N_SEQ, width).astype(jnp.float32), w_out.reshape(N_SEQ, width, D).astype(jnp.float32))
    partial_value = lax.optimization_barrier(partial_value.astype(jnp.bfloat16)).astype(jnp.float32)
    attended = lax.optimization_barrier(jnp.sum(partial_value, axis=0))
    result = (hidden.astype(jnp.float32) + mods[2] * attended).astype(jnp.bfloat16)
    return (result, keys, values)

def reference(patches, qkv_weight, out_weight, modulation, stale_keys, stale_values, offsets):
    current = patches
    keys = stale_keys
    values = stale_values
    for step in range(TICKS):

        def one_section(section_args):
            hidden, w_qkv, w_out, mods, cache_k, cache_v, slots = section_args
            return layer(hidden, w_qkv, w_out, mods, cache_k, cache_v, slots[step])
        result, keys, values = lax.map(one_section, (current, qkv_weight, out_weight, modulation, keys, values, offsets))
        if step + 1 < TICKS:
            current = jnp.roll(result, 1, axis=0)
        else:
            current = result
    return current
```

```python
import functools
import math

import jax
import jax.numpy as jnp
from jax import lax
from jax.experimental import pallas as pl
from jax.experimental.pallas import tpu as pltpu
from jax.sharding import PartitionSpec as P

HEAD_DIM = 72
TICKS = 2
AXES = ("pipe", "seq")
EXPONENT = math.log2(math.e) / math.sqrt(HEAD_DIM)


def partner(kind, section, member):
    if (kind + section) % 2 == 0:
        return member ^ 1
    return 3 - member


def exchange(array, kind, by=0):
    sections, members = lax.axis_size("pipe"), lax.axis_size("seq")
    moves = []
    for section in range(sections):
        target = (section + by) % sections
        for member in range(members):
            source = member if kind is None else partner(kind, target, member)
            moves.append((section * members + source, target * members + member))
    return lax.ppermute(array, AXES, moves)


def dot(a, b, contract_a, contract_b):
    return lax.dot_general(
        a, b, (((contract_a,), (contract_b,)), ((), ())), preferred_element_type=jnp.float32
    )


def normalize(rows, shift, scale):
    values = rows.astype(jnp.float32)
    center = jnp.mean(values, axis=-1, keepdims=True)
    values = values - center
    spread = jnp.mean(values * values, axis=-1, keepdims=True)
    return (values * lax.rsqrt(spread + 1e-06) * (1.0 + scale) + shift).astype(jnp.bfloat16)


def block_kernel(
    own_ref, one_ref, two_ref, far_a_ref, far_b_ref, mods_ref, w_ref, ko_ref, vo_ref, wo_ref,
    p_own, p_one_a, p_one_b, p_two_a, p_two_b, p_far_a, p_far_b, kn_ref, vn_ref,
    normed, qkv, mixed,
):
    rows = own_ref.shape[0]
    half = rows // 2
    width = wo_ref.shape[0]
    at = 0
    for ref in (own_ref, one_ref, two_ref, far_a_ref, far_b_ref):
        normed[at : at + ref.shape[0]] = normalize(ref[...], mods_ref[0:1], mods_ref[1:2])
        at += ref.shape[0]
    qkv[...] = dot(w_ref[...], normed[...], 1, 1)
    kn_ref[...] = qkv[width : 2 * width].astype(jnp.bfloat16)
    vn_ref[...] = qkv[2 * width :].astype(jnp.bfloat16)
    ko = ko_ref[...].astype(jnp.float32)
    vo = vo_ref[...].astype(jnp.float32)
    for h in range(width // HEAD_DIM):
        lo, hi = h * HEAD_DIM, (h + 1) * HEAD_DIM
        q = qkv[lo:hi].astype(jnp.bfloat16)
        kn = qkv[width + lo : width + hi].astype(jnp.bfloat16)
        vn = qkv[2 * width + lo : 2 * width + hi].astype(jnp.bfloat16)
        s1 = dot(kn, q, 0, 0)
        s2 = dot(ko[lo:hi].astype(jnp.bfloat16), q, 0, 0)
        top = jnp.maximum(jnp.max(s1, 0, keepdims=True), jnp.max(s2, 0, keepdims=True))
        e1 = jnp.exp2((s1 - top) * EXPONENT)
        e2 = jnp.exp2((s2 - top) * EXPONENT)
        total = jnp.sum(e1, 0, keepdims=True) + jnp.sum(e2, 0, keepdims=True)
        out = dot(vn, e1.astype(jnp.bfloat16), 1, 0)
        out += dot(vo[lo:hi].astype(jnp.bfloat16), e2.astype(jnp.bfloat16), 1, 0)
        mixed[lo:hi] = out * (1.0 / total)
    partial = dot(mixed[...].astype(jnp.bfloat16), wo_ref[...], 0, 0)
    p_own[...] = partial[:rows]
    at = rows
    for ref in (p_one_a, p_one_b, p_two_a, p_two_b, p_far_a, p_far_b):
        ref[...] = partial[at : at + half].astype(jnp.bfloat16)
        at += half


def block(parts, mods, w, ko, vo, wo):
    rows, features = parts[0].shape
    half = rows // 2
    count = rows * 4
    width = wo.shape[0]
    piece = jax.ShapeDtypeStruct((half, features), jnp.bfloat16)
    cache = jax.ShapeDtypeStruct((width, count), jnp.bfloat16)
    return pl.pallas_call(
        block_kernel,
        out_shape=[jax.ShapeDtypeStruct((rows, features), jnp.float32)] + [piece] * 6 + [cache] * 2,
        scratch_shapes=[
            pltpu.VMEM((count, features), jnp.bfloat16),
            pltpu.VMEM((3 * width, count), jnp.float32),
            pltpu.VMEM((width, count), jnp.float32),
        ],
        compiler_params=pltpu.CompilerParams(vmem_limit_bytes=40 * 2**20),
        cost_estimate=pl.CostEstimate(
            flops=2 * count * features * width * 4 + 8 * count * count * width,
            bytes_accessed=8 * 2**20,
            transcendentals=8 * count * count,
        ),
    )(*parts, mods, w, ko, vo, wo)


def gathered(rows, by):
    half = rows.shape[0] // 2
    two = exchange(rows, 1, by)
    one = exchange(rows, 0, by)
    own = exchange(rows, None, by) if by else rows
    far_a = exchange(two[:half], 0)
    far_b = exchange(one[half:], 1)
    return own, one, two, far_a, far_b


def summed(own, one_a, one_b, two_a, two_b, far_a, far_b):
    from_one = exchange(far_a, 0)
    from_two = exchange(far_b, 1)
    early_a = exchange(one_a, 0)
    early_b = exchange(two_b, 1)
    late_b = exchange(one_b + from_two, 0)
    late_a = exchange(two_a + from_one, 1)
    others_a = early_a.astype(jnp.float32) + late_a.astype(jnp.float32)
    others_b = early_b.astype(jnp.float32) + late_b.astype(jnp.float32)
    return own + jnp.concatenate([others_a, others_b], axis=0)


def body(patches, qkv_weight, out_weight, modulation, stale_keys, stale_values, offsets):
    width = qkv_weight.shape[3]
    features = qkv_weight.shape[1]
    w = jnp.transpose(qkv_weight[0], (1, 2, 0)).reshape(3 * width, features)
    wo = out_weight[0]
    mods = modulation[0]
    gate = mods[2]
    keys = jnp.transpose(stale_keys[0])
    values = jnp.transpose(stale_values[0])
    count = patches.shape[1] * lax.axis_size("seq")

    def kept(cache, step):
        return lax.dynamic_slice(cache, (0, (1 - offsets[0, step]) * count), (width, count))

    current = patches[0]
    parts = gathered(current, 0)
    ko, vo = kept(keys, 0), kept(values, 0)
    for step in range(TICKS):
        *partial, kn, vn = block(parts, mods, w, ko, vo, wo)
        hidden = parts[0].astype(jnp.float32) + gate * summed(*partial)
        current = hidden.astype(jnp.bfloat16)
        if step + 1 < TICKS:
            same = offsets[0, step] == offsets[0, step + 1]
            ko = jnp.where(same, kept(keys, step + 1), kn)
            vo = jnp.where(same, kept(values, step + 1), vn)
            parts = gathered(current, 1)
    return current[None]


def solution(mesh):
    placed = (
        P("pipe", "seq", None),
        P("pipe", None, None, "seq"),
        P("pipe", "seq", None),
        P("pipe", None, None),
        P("pipe", None, "seq"),
        P("pipe", None, "seq"),
        P("pipe", None),
    )
    return jax.shard_map(
        body, mesh=mesh, in_specs=placed, out_specs=P("pipe", "seq", None), check_vma=False
    )
```

```python
import functools
import math

import jax
import jax.numpy as jnp
from jax import lax
from jax.experimental import pallas as pl
from jax.experimental.pallas import tpu as pltpu
from jax.sharding import PartitionSpec as P

HEAD_DIM = 72
AXES = ("pipe", "seq")
VMEM_BYTES = 24 * 2**20
EXPONENT = math.log2(math.e) / math.sqrt(HEAD_DIM)


def partner(kind, section, member):
    if kind == 2:
        return member ^ 2
    if (kind + section) % 2 == 0:
        return member ^ 1
    return 3 - member


def exchange(array, kind):
    sections, members = lax.axis_size("pipe"), lax.axis_size("seq")
    moves = []
    for section in range(sections):
        for member in range(members):
            moves.append((section * members + partner(kind, section, member), section * members + member))
    return lax.ppermute(array, AXES, moves)


def advance(array, kind):
    sections, members = lax.axis_size("pipe"), lax.axis_size("seq")
    moves = []
    for section in range(sections):
        target = (section + 1) % sections
        for member in range(members):
            place = member if kind is None else partner(kind, section, member)
            moves.append((section * members + member, target * members + place))
    return lax.ppermute(array, AXES, moves)


def dot(a, b, contract_a, contract_b):
    return lax.dot_general(
        a, b, (((contract_a,), (contract_b,)), ((), ())), preferred_element_type=jnp.float32
    )


def normalize(rows, shift, scale):
    values = rows.astype(jnp.float32)
    center = jnp.mean(values, axis=-1, keepdims=True)
    values = values - center
    spread = jnp.mean(values * values, axis=-1, keepdims=True)
    return (values * lax.rsqrt(spread + 1e-06) * (1.0 + scale) + shift).astype(jnp.bfloat16)


def weighted(queries, caches, prior=None):
    scores = [dot(keys, queries, 0, 0) for keys, _ in caches]
    top = functools.reduce(jnp.maximum, [jnp.max(s, 0, keepdims=True) for s in scores])
    total = out = 0.0
    if prior is not None:
        top = jnp.maximum(top, prior[0])
        shrink = jnp.exp2((prior[0] - top) * EXPONENT)
        total, out = prior[1] * shrink, prior[2] * shrink
    for s, (_, values) in zip(scores, caches, strict=True):
        weights = jnp.exp2((s - top) * EXPONENT)
        total = total + jnp.sum(weights, 0, keepdims=True)
        out = out + dot(values, weights.astype(jnp.bfloat16), 1, 0)
    return top, total, out


def head_of(ref_or_array, h):
    return ref_or_array[h * HEAD_DIM : (h + 1) * HEAD_DIM]


def project_qkv(parts, mods_ref, w_ref, normed, qkv):
    at = 0
    for ref in parts:
        normed[at : at + ref.shape[0]] = normalize(ref[...], mods_ref[0:1], mods_ref[1:2])
        at += ref.shape[0]
    qkv[...] = dot(w_ref[...], normed[...], 1, 1)


def early_kernel(step, n_parts, *refs):
    parts, refs = refs[:n_parts], refs[n_parts:]
    n_olds = 4 if step else 0
    olds, refs = refs[:n_olds], refs[n_olds:]
    (offsets_ref, mods_ref, w_ref, stale_k_ref, stale_v_ref,
     q_ref, k_ref, v_ref, ko_ref, vo_ref, top_ref, total_ref, out_ref, normed, qkv) = refs
    width, count = ko_ref.shape
    start = pl.multiple_of((1 - offsets_ref[step]) * count, count)
    ko_ref[...] = stale_k_ref[:, pl.ds(start, count)]
    vo_ref[...] = stale_v_ref[:, pl.ds(start, count)]
    if step:
        @pl.when(offsets_ref[0] != offsets_ref[step])
        def _():
            split = olds[0].shape[1]
            ko_ref[:, :split] = olds[0][...]
            ko_ref[:, split:] = olds[1][...]
            vo_ref[:, :split] = olds[2][...]
            vo_ref[:, split:] = olds[3][...]

    project_qkv(parts, mods_ref, w_ref, normed, qkv)
    q_ref[...] = qkv[:width].astype(jnp.bfloat16)
    k_ref[...] = qkv[width : 2 * width].astype(jnp.bfloat16)
    v_ref[...] = qkv[2 * width :].astype(jnp.bfloat16)
    ko = ko_ref[...].astype(jnp.float32)
    vo = vo_ref[...].astype(jnp.float32)
    for h in range(width // HEAD_DIM):
        lo, hi = h * HEAD_DIM, (h + 1) * HEAD_DIM
        top, total, out = weighted(
            qkv[lo:hi].astype(jnp.bfloat16),
            [
                (qkv[width + lo : width + hi].astype(jnp.bfloat16), qkv[2 * width + lo : 2 * width + hi].astype(jnp.bfloat16)),
                (ko[lo:hi].astype(jnp.bfloat16), vo[lo:hi].astype(jnp.bfloat16)),
            ],
        )
        top_ref[h : h + 1] = top
        total_ref[h : h + 1] = total
        out_ref[lo:hi] = out


def early(step, parts, olds, offsets, mods, w, stale_k, stale_v):
    rows = sum(part.shape[0] for part in parts)
    features = parts[0].shape[1]
    width, count = stale_k.shape[0], stale_k.shape[1] // 2
    narrow = jax.ShapeDtypeStruct((width, rows), jnp.bfloat16)
    half = jax.ShapeDtypeStruct((width, count), jnp.bfloat16)
    stat = jax.ShapeDtypeStruct((8, rows), jnp.float32)
    vmem = pl.BlockSpec(memory_space=pltpu.VMEM)
    return pl.pallas_call(
        functools.partial(early_kernel, step, len(parts)),
        out_shape=[narrow, narrow, narrow, half, half, stat, stat, jax.ShapeDtypeStruct((width, rows), jnp.float32)],
        in_specs=[vmem] * (len(parts) + len(olds)) + [pl.BlockSpec(memory_space=pltpu.SMEM)] + [vmem] * 4,
        scratch_shapes=[pltpu.VMEM((rows, features), jnp.bfloat16), pltpu.VMEM((3 * width, rows), jnp.float32)],
        compiler_params=pltpu.CompilerParams(vmem_limit_bytes=VMEM_BYTES),
        cost_estimate=pl.CostEstimate(
            flops=2 * rows * features * width * 3 + 4 * rows * (rows + count) * width,
            bytes_accessed=4 * 2**20,
            transcendentals=4 * rows * (rows + count),
        ),
    )(*parts, *olds, offsets, mods, w, stale_k, stale_v)


def merge_heads(target, pieces, early_refs, late, ko_ref, vo_ref):
    q_ref, k_ref, v_ref, top_ref, total_ref, out_ref = early_refs
    width = k_ref.shape[0]
    f32 = [ref[...].astype(jnp.float32) for ref in (q_ref, k_ref, v_ref, ko_ref, vo_ref)]
    for h in range(width // HEAD_DIM):
        qe, ke, ve, ko, vo = (head_of(a, h).astype(jnp.bfloat16) for a in f32)
        ql, kl, vl = (head_of(a, h).astype(jnp.bfloat16) for a in late)
        at = 0
        for is_early, first, last in pieces:
            if is_early:
                prior = (
                    top_ref[h : h + 1, first:last],
                    total_ref[h : h + 1, first:last],
                    out_ref[h * HEAD_DIM : (h + 1) * HEAD_DIM, first:last],
                )
                _, total, out = weighted(qe[:, first:last], [(kl, vl)], prior)
            else:
                _, total, out = weighted(ql[:, first:last], [(ke, ve), (ko, vo), (kl, vl)])
            target[h * HEAD_DIM : (h + 1) * HEAD_DIM, at : at + last - first] = out * (1.0 / total)
            at += last - first


def late_kernel(n_parts, pieces, *refs):
    parts, refs = refs[:n_parts], refs[n_parts:]
    mods_ref, w_ref, ko_ref, vo_ref, *early_refs = refs[:10]
    sent_ref, q_ref, k_ref, v_ref, normed, qkv, mixed = refs[10:]
    width = ko_ref.shape[0]
    project_qkv(parts, mods_ref, w_ref, normed, qkv)
    q_ref[...] = qkv[:width].astype(jnp.bfloat16)
    k_ref[...] = qkv[width : 2 * width].astype(jnp.bfloat16)
    v_ref[...] = qkv[2 * width :].astype(jnp.bfloat16)
    merge_heads(mixed, pieces, early_refs, (qkv[:width], qkv[width : 2 * width], qkv[2 * width :]), ko_ref, vo_ref)
    sent_ref[...] = mixed[...].astype(jnp.bfloat16)


def work(pieces, count, width):
    return 4 * sum(last - first for _, first, last in pieces) * count * width


def late(parts, pieces, mods, w, ko, vo, early_state):
    rows = sum(part.shape[0] for part in parts)
    features = parts[0].shape[1]
    width, count = ko.shape
    columns = sum(last - first for _, first, last in pieces)
    narrow = jax.ShapeDtypeStruct((width, rows), jnp.bfloat16)
    return pl.pallas_call(
        functools.partial(late_kernel, len(parts), pieces),
        out_shape=[jax.ShapeDtypeStruct((width, columns), jnp.bfloat16), narrow, narrow, narrow],
        scratch_shapes=[
            pltpu.VMEM((rows, features), jnp.bfloat16),
            pltpu.VMEM((3 * width, rows), jnp.float32),
            pltpu.VMEM((width, columns), jnp.float32),
        ],
        compiler_params=pltpu.CompilerParams(vmem_limit_bytes=VMEM_BYTES),
        cost_estimate=pl.CostEstimate(
            flops=2 * rows * features * width * 3 + work(pieces, count, width),
            bytes_accessed=4 * 2**20,
            transcendentals=4 * columns * count,
        ),
    )(*parts, mods, w, ko, vo, *early_state)


def rest_kernel(pieces, *refs):
    ko_ref, vo_ref, *early_refs = refs[:8]
    ql_ref, kl_ref, vl_ref, kept_ref, mixed = refs[8:]
    late_arrays = [ref[...].astype(jnp.float32) for ref in (ql_ref, kl_ref, vl_ref)]
    merge_heads(mixed, pieces, early_refs, late_arrays, ko_ref, vo_ref)
    kept_ref[...] = mixed[...].astype(jnp.bfloat16)


def rest(pieces, ko, vo, early_state, late_state):
    width, count = ko.shape
    columns = sum(last - first for _, first, last in pieces)
    return pl.pallas_call(
        functools.partial(rest_kernel, pieces),
        out_shape=jax.ShapeDtypeStruct((width, columns), jnp.bfloat16),
        scratch_shapes=[pltpu.VMEM((width, columns), jnp.float32)],
        compiler_params=pltpu.CompilerParams(vmem_limit_bytes=VMEM_BYTES),
        cost_estimate=pl.CostEstimate(
            flops=work(pieces, count, width), bytes_accessed=3 * 2**20, transcendentals=4 * columns * count
        ),
    )(ko, vo, *early_state, *late_state)


def project_kernel(mine_ref, theirs_ref, w_mine_ref, w_theirs_ref, *out_refs):
    total = dot(mine_ref[...], w_mine_ref[...], 0, 0) + dot(theirs_ref[...], w_theirs_ref[...], 0, 0)
    rows = out_refs[0].shape[0]
    for i, ref in enumerate(out_refs):
        ref[...] = total[i * rows : (i + 1) * rows].astype(jnp.bfloat16)


def project(mine, theirs, w_mine, w_theirs):
    rows, features, width = mine.shape[1], w_mine.shape[1], mine.shape[0]
    return pl.pallas_call(
        project_kernel,
        out_shape=[jax.ShapeDtypeStruct((rows // 2, features), jnp.bfloat16)] * 2,
        compiler_params=pltpu.CompilerParams(vmem_limit_bytes=VMEM_BYTES),
        cost_estimate=pl.CostEstimate(
            flops=4 * rows * features * width, bytes_accessed=3 * 2**20, transcendentals=0
        ),
    )(mine, theirs, w_mine, w_theirs)


def update_kernel(hidden_ref, mods_ref, mine_ref, theirs_ref, out_ref):
    attended = mine_ref[...].astype(jnp.float32) + theirs_ref[...].astype(jnp.float32)
    out_ref[...] = (hidden_ref[...].astype(jnp.float32) + mods_ref[2:3] * attended).astype(jnp.bfloat16)


def update(hidden, mods, mine, theirs):
    return pl.pallas_call(
        update_kernel,
        out_shape=jax.ShapeDtypeStruct(hidden.shape, jnp.bfloat16),
        compiler_params=pltpu.CompilerParams(vmem_limit_bytes=VMEM_BYTES),
        cost_estimate=pl.CostEstimate(flops=4 * hidden.size, bytes_accessed=8 * hidden.size, transcendentals=0),
    )(hidden, mods, mine, theirs)


def body(patches, qkv_weight, out_weight, modulation, stale_keys, stale_values, offsets):
    width = qkv_weight.shape[3]
    features = qkv_weight.shape[1]
    w = jnp.transpose(qkv_weight[0], (1, 2, 0)).reshape(3 * width, features)
    w_mine = out_weight[0]
    mods = modulation[0]
    stale = (jnp.transpose(stale_keys[0]), jnp.transpose(stale_values[0]))
    slots = offsets[0]
    own = patches[0]
    rows = own.shape[0]

    with jax.named_scope("first_gather"):
        zero = exchange(own, 0)
        one = exchange(own, 1)
        far = exchange(zero, 1)
    w_sent, zero, one = lax.optimization_barrier((w_mine, zero, one))
    with jax.named_scope("first_tick"):
        q, k, v, ko, vo, *stats = early(0, (zero, own, one), (), slots, mods, w, *stale)
        w_theirs = exchange(w_sent, 0)
        state = (q, k, v, *stats)
        sent, *late_state = late((far,), ((True, 0, rows), (False, 0, rows)), mods, w, ko, vo, state)
        theirs = exchange(sent, 0)
        kept = rest(((True, rows, 3 * rows),), ko, vo, state, late_state)
        mine_own, mine_one = project(kept, theirs, w_mine, w_theirs)
        olds = (k, late_state[1], v, late_state[2])
    with jax.named_scope("sum_and_shift"):
        next_one = update(one, mods, mine_one, exchange(mine_own, 1))
        next_own = update(own, mods, mine_own, exchange(mine_one, 1))
        straight_one, crossing_one = advance(next_one, None), advance(next_one, 0)
        straight_own, crossing_own = advance(next_own, None), advance(next_own, 0)
    with jax.named_scope("second_tick"):
        q, k, v, ko, vo, *stats = early(1, (straight_one, crossing_one), olds, slots, mods, w, *stale)
        state = (q, k, v, *stats)
        sent, *late_state = late((straight_own, crossing_own), ((True, 0, 2 * rows),), mods, w, ko, vo, state)
        theirs = exchange(sent, 0)
        kept = rest(((False, 0, 2 * rows),), ko, vo, state, late_state)
        mine_own, mine_one = project(kept, theirs, w_mine, w_theirs)
        return update(straight_own, mods, mine_own, exchange(mine_one, 1))[None]


def solution(mesh):
    placed = (
        P("pipe", "seq", None),
        P("pipe", None, None, "seq"),
        P("pipe", "seq", None),
        P("pipe", None, None),
        P("pipe", None, "seq"),
        P("pipe", None, "seq"),
        P("pipe", None),
    )
    return jax.shard_map(
        body, mesh=mesh, in_specs=placed, out_specs=P("pipe", "seq", None), check_vma=False
    )
```

```python
import functools
import math

import jax
import jax.numpy as jnp
from jax import lax
from jax.experimental import pallas as pl
from jax.experimental.pallas import tpu as pltpu
from jax.sharding import PartitionSpec as P

HEAD_DIM = 72
AXES = ("pipe", "seq")
VMEM_BYTES = 24 * 2**20
EXPONENT = math.log2(math.e) / math.sqrt(HEAD_DIM)


def partner(kind, section, member):
    if kind == 2:
        return member ^ 2
    if (kind + section) % 2 == 0:
        return member ^ 1
    return 3 - member


def exchange(array, kind):
    sections, members = lax.axis_size("pipe"), lax.axis_size("seq")
    moves = []
    for section in range(sections):
        for member in range(members):
            moves.append((section * members + partner(kind, section, member), section * members + member))
    return lax.ppermute(array, AXES, moves)


def advance(array, kind):
    sections, members = lax.axis_size("pipe"), lax.axis_size("seq")
    moves = []
    for section in range(sections):
        target = (section + 1) % sections
        for member in range(members):
            place = member if kind is None else partner(kind, section, member)
            moves.append((section * members + member, target * members + place))
    return lax.ppermute(array, AXES, moves)


def dot(a, b, contract_a, contract_b):
    return lax.dot_general(
        a, b, (((contract_a,), (contract_b,)), ((), ())), preferred_element_type=jnp.float32
    )


def normalize(rows, shift, scale):
    values = rows.astype(jnp.float32)
    center = jnp.mean(values, axis=-1, keepdims=True)
    values = values - center
    spread = jnp.mean(values * values, axis=-1, keepdims=True)
    return (values * lax.rsqrt(spread + 1e-06) * (1.0 + scale) + shift).astype(jnp.bfloat16)


def split_heads(source, refs):
    at = 0
    for ref in refs:
        for h in range(ref.shape[0]):
            ref[h] = source[at : at + HEAD_DIM].astype(jnp.bfloat16)
            at += HEAD_DIM


def attend(heads, jobs):
    scored = []
    for h in range(heads):
        for queries, caches, prior, store in jobs:
            q, pairs = queries(h), caches(h)
            scored.append((h, [dot(keys, q, 0, 0) for keys, _ in pairs], pairs, prior, store))
    for h, scores, pairs, prior, store in scored:
        top = functools.reduce(jnp.maximum, [jnp.max(s, 0, keepdims=True) for s in scores])
        total = out = 0.0
        if prior is not None:
            old_top, old_total, old_out = prior(h)
            top = jnp.maximum(top, old_top)
            shrink = jnp.exp2((old_top - top) * EXPONENT)
            total, out = old_total * shrink, old_out * shrink
        for s, (_, values) in zip(scores, pairs, strict=True):
            weights = jnp.exp2((s - top) * EXPONENT)
            total = total + jnp.sum(weights, 0, keepdims=True)
            out = out + dot(values, weights.astype(jnp.bfloat16), 1, 0)
        store(h, top, total, out)


def call(kernel, outs, scratch, flops, exps, operands, smem=()):
    specs = [pl.BlockSpec(memory_space=pltpu.SMEM if i in smem else pltpu.VMEM) for i in range(len(operands))]
    return pl.pallas_call(
        kernel,
        out_shape=outs,
        in_specs=specs,
        scratch_shapes=scratch,
        compiler_params=pltpu.CompilerParams(vmem_limit_bytes=VMEM_BYTES),
        cost_estimate=pl.CostEstimate(flops=flops, bytes_accessed=4 * 2**20, transcendentals=exps),
    )(*operands)


def shape(dtype, *sizes):
    return jax.ShapeDtypeStruct(sizes, dtype)


def prepare_kernel(offsets_ref, mods_ref, w_ref, wo_ref, stale_k_ref, stale_v_ref, mods_out, w_out, wo_out, *kept):
    mods_out[...] = mods_ref[...]
    w_out[...] = w_ref[...]
    wo_out[...] = wo_ref[...]
    count = kept[0].shape[2]
    for step in range(2):
        start = pl.multiple_of((1 - offsets_ref[step]) * count, count)
        for stale_ref, ref in zip((stale_k_ref, stale_v_ref), kept[2 * step : 2 * step + 2], strict=True):
            split_heads(stale_ref[:, pl.ds(start, count)].astype(jnp.float32), (ref,))


def prepare(offsets, mods, w, wo, stale_k, stale_v):
    width, context = stale_k.shape
    half = shape(jnp.bfloat16, width // HEAD_DIM, HEAD_DIM, context // 2)
    same = [shape(a.dtype, *a.shape) for a in (mods, w, wo)]
    return call(prepare_kernel, same + [half] * 4, [], 0, 0, (offsets, mods, w, wo, stale_k, stale_v), (0,))


def load_rows(refs, places, mods_ref, w_ref, normed, qkv):
    at = 0
    for i, first, last in places:
        normed[at : at + last - first] = normalize(refs[i][first:last], mods_ref[0:1], mods_ref[1:2])
        at += last - first
    qkv[...] = dot(w_ref[...], normed[...], 1, 1)


def early_kernel(places, n_parts, n_olds, *refs):
    parts, refs = refs[:n_parts], refs[n_parts:]
    olds, refs = refs[:n_olds], refs[n_olds:]
    mods_ref, w_ref, ko_ref, vo_ref, *outs, normed, qkv = refs
    q_ref, k_ref, v_ref, top_ref, total_ref, out_ref, *chosen = outs
    if olds:
        offsets_ref, *olds = olds
        for stale_ref, ref, old in zip((ko_ref, vo_ref), chosen, (olds[:2], olds[2:]), strict=True):
            ref[...] = stale_ref[...]

            @pl.when(offsets_ref[0] != offsets_ref[1])
            def _(ref=ref, old=old):
                split = old[0].shape[2]
                ref[:, :, :split] = old[0][...]
                ref[:, :, split:] = old[1][...]

        ko_ref, vo_ref = chosen
    load_rows(parts, places, mods_ref, w_ref, normed, qkv)
    split_heads(qkv, (q_ref, k_ref, v_ref))

    def store(h, top, total, out):
        top_ref[h : h + 1] = top
        total_ref[h : h + 1] = total
        out_ref[h] = out

    heads = q_ref.shape[0]
    attend(heads, [(lambda h: q_ref[h], lambda h: [(k_ref[h], v_ref[h]), (ko_ref[h], vo_ref[h])], None, store)])


def early(parts, places, olds, mods, w, ko, vo):
    rows, features = sum(last - first for _, first, last in places), w.shape[1]
    heads, _, count = ko.shape
    block = shape(jnp.bfloat16, heads, HEAD_DIM, rows)
    stat = shape(jnp.float32, 8, rows)
    chosen = [shape(jnp.bfloat16, *ko.shape)] * 2 if olds else []
    return call(
        functools.partial(early_kernel, places, len(parts), len(olds)),
        [block] * 3 + [stat, stat, shape(jnp.float32, heads, HEAD_DIM, rows)] + chosen,
        [pltpu.VMEM((rows, features), jnp.bfloat16), pltpu.VMEM((w.shape[0], rows), jnp.float32)],
        2 * rows * features * w.shape[0] + 4 * rows * (rows + count) * heads * HEAD_DIM,
        heads * rows * (rows + count), (*parts, *olds, mods, w, ko, vo), (len(parts),) if olds else (),
    )


def merge_job(mixed, at, span, early_refs, late_refs):
    q_ref, _, _, top_ref, total_ref, out_ref = early_refs
    _, kl_ref, vl_ref = late_refs
    first, last = span

    def store(h, top, total, out):
        mixed[h * HEAD_DIM : (h + 1) * HEAD_DIM, at : at + last - first] = out * (1.0 / total)

    return (
        lambda h: q_ref[h, :, first:last],
        lambda h: [(kl_ref[h], vl_ref[h])],
        lambda h: (top_ref[h : h + 1, first:last], total_ref[h : h + 1, first:last], out_ref[h, :, first:last]),
        store,
    )


def whole_job(mixed, at, span, early_refs, late_refs, ko_ref, vo_ref):
    _, k_ref, v_ref, *_ = early_refs
    ql_ref, kl_ref, vl_ref = late_refs
    first, last = span

    def store(h, top, total, out):
        mixed[h * HEAD_DIM : (h + 1) * HEAD_DIM, at : at + last - first] = out * (1.0 / total)

    return (
        lambda h: ql_ref[h, :, first:last],
        lambda h: [(k_ref[h], v_ref[h]), (ko_ref[h], vo_ref[h]), (kl_ref[h], vl_ref[h])],
        None,
        store,
    )


def finish(mixed, span, early_refs, late_refs, ko_ref, vo_ref):
    size = span[1] - span[0]
    attend(
        ko_ref.shape[0],
        [
            merge_job(mixed, 0, span, early_refs, late_refs),
            whole_job(mixed, size, span, early_refs, late_refs, ko_ref, vo_ref),
        ],
    )


def late_kernel(places, n_parts, *refs):
    parts, refs = refs[:n_parts], refs[n_parts:]
    mods_ref, w_ref, ko_ref, vo_ref, *early_refs = refs[:10]
    sent_ref, *late_refs, normed, qkv, mixed = refs[10:]
    load_rows(parts, places, mods_ref, w_ref, normed, qkv)
    split_heads(qkv, late_refs)
    finish(mixed, (0, mixed.shape[1] // 2), early_refs, late_refs, ko_ref, vo_ref)
    sent_ref[...] = mixed[...].astype(jnp.bfloat16)


def late(parts, places, mods, w, ko, vo, early_state):
    rows, features = sum(last - first for _, first, last in places), w.shape[1]
    heads, _, count = ko.shape
    width = heads * HEAD_DIM
    return call(
        functools.partial(late_kernel, places, len(parts)),
        [shape(jnp.bfloat16, width, rows)] + [shape(jnp.bfloat16, heads, HEAD_DIM, rows)] * 3,
        [
            pltpu.VMEM((rows, features), jnp.bfloat16),
            pltpu.VMEM((w.shape[0], rows), jnp.float32),
            pltpu.VMEM((width, rows), jnp.float32),
        ],
        2 * rows * features * w.shape[0] + 4 * rows * count * width,
        heads * rows * count, (*parts, mods, w, ko, vo, *early_state),
    )


def rest_kernel(ko_ref, vo_ref, *refs):
    early_refs, late_refs, (kept_ref, mixed) = refs[:6], refs[6:9], refs[9:]
    columns = mixed.shape[1]
    finish(mixed, (columns // 2, columns), early_refs, late_refs, ko_ref, vo_ref)
    kept_ref[...] = mixed[...].astype(jnp.bfloat16)


def rest(ko, vo, early_state, late_state):
    heads, _, count = ko.shape
    width, rows = heads * HEAD_DIM, late_state[0].shape[2]
    return call(
        rest_kernel, shape(jnp.bfloat16, width, rows), [pltpu.VMEM((width, rows), jnp.float32)],
        64 * 4 * rows * count * width, heads * rows * count, (ko, vo, *early_state, *late_state),
    )


def block(early_parts, late_parts, places, olds, mods, w, ko, vo, also=()):
    state = early(early_parts, places[0], olds, mods, w, ko, vo)
    if olds:
        *state, ko, vo = state
    sent, *late_state = late(late_parts, places[1], mods, w, ko, vo, state)
    theirs = exchange(sent, 0)
    mine = rest(ko, vo, state, late_state)
    return mine, theirs, (state[1], late_state[1], state[2], late_state[2]), also


def both_sums(mine_ref, theirs_ref, w_mine_ref, w_theirs_ref):
    return dot(mine_ref[...], w_mine_ref[...], 0, 0) + dot(theirs_ref[...], w_theirs_ref[...], 0, 0)


def shift_kernel(spans, own_ref, other_a, other_b, mods_ref, *refs):
    *refs, straight_a, crossing_a, straight_b, crossing_b = refs
    half = straight_a.shape[0] // 2
    added = mods_ref[2:3] * both_sums(*refs)
    chunks = ((other_a, straight_a, crossing_a), (other_b, straight_b, crossing_b))
    for i, ((first, last), (other, straight, crossing)) in enumerate(zip(spans, chunks, strict=True)):
        at = 2 * i * half
        own, one = added[at : at + half], added[at + half : at + 2 * half]
        straight[:half] = (own_ref[first:last].astype(jnp.float32) + own).astype(jnp.bfloat16)
        straight[half:] = (other[:half].astype(jnp.float32) + one).astype(jnp.bfloat16)
        crossing[:half] = one.astype(jnp.bfloat16)
        crossing[half:] = own.astype(jnp.bfloat16)


def shift(spans, own, others, mods, mine, theirs, w_mine, w_theirs):
    rows, features, width = mine.shape[1], w_mine.shape[1], mine.shape[0]
    return call(
        functools.partial(shift_kernel, spans), [shape(jnp.bfloat16, rows // 2, features)] * 4, [],
        4 * rows * features * width, 0, (own, *others, mods, mine, theirs, w_mine, w_theirs),
    )


def join_kernel(crossing_ref, straight_ref, out_ref):
    total = straight_ref[...].astype(jnp.float32) + crossing_ref[...].astype(jnp.float32)
    out_ref[...] = total.astype(jnp.bfloat16)


def join(crossing, straight):
    return call(join_kernel, shape(straight.dtype, *straight.shape), [], straight.size, 0, (crossing, straight))


def last_kernel(*refs):
    *refs, kept_ref, sent_ref = refs
    rows = kept_ref.shape[0]
    total = both_sums(*refs)
    kept_ref[...] = total[:rows]
    sent_ref[...] = total[rows:].astype(jnp.bfloat16)


def project_last(mine, theirs, w_mine, w_theirs):
    rows, features, width = mine.shape[1] // 2, w_mine.shape[1], mine.shape[0]
    return call(
        last_kernel, [shape(jnp.float32, rows, features), shape(jnp.bfloat16, rows, features)], [],
        8 * rows * features * width, 0, (mine, theirs, w_mine, w_theirs),
    )


def update_kernel(places, n_parts, mods_ref, *refs):
    parts, (mine_ref, theirs_ref, out_ref) = refs[:n_parts], refs[n_parts:]
    attended = mine_ref[...].astype(jnp.float32) + theirs_ref[...].astype(jnp.float32)
    at = 0
    for i, first, last in places:
        here = slice(at, at + last - first)
        new = parts[i][first:last].astype(jnp.float32) + mods_ref[2:3] * attended[here]
        out_ref[here] = new.astype(jnp.bfloat16)
        at += last - first


def update(parts, places, mods, mine, theirs):
    return call(
        functools.partial(update_kernel, places, len(parts)),
        shape(jnp.bfloat16, *mine.shape), [], 4 * mine.size, 0, (mods, *parts, mine, theirs),
    )


def pack_kernel(first, last, own_ref, zero_ref, out_ref):
    half = last - first
    out_ref[:half] = own_ref[first:last]
    out_ref[half:] = zero_ref[...]


def pack(own, first, last, zero):
    return call(
        functools.partial(pack_kernel, first, last),
        shape(own.dtype, 2 * (last - first), own.shape[1]), [], 0, 0, (own, zero),
    )


def body(patches, qkv_weight, out_weight, modulation, stale_keys, stale_values, offsets):
    width = qkv_weight.shape[3]
    features = qkv_weight.shape[1]
    w = jnp.transpose(qkv_weight[0], (1, 2, 0)).reshape(3 * width, features)
    w_sent = out_weight[0]
    slots = offsets[0]
    own = patches[0]
    rows = own.shape[0]
    half = rows // 2
    spans = ((0, half), (half, rows))

    with jax.named_scope("first_gather"):
        zeros = [exchange(own[first:last], 0) for first, last in spans]
        packed = [pack(own, *span, zero) for span, zero in zip(spans, zeros, strict=True)]
        others = [exchange(rows_here, 1) for rows_here in packed]
        w_sent, *_ = lax.optimization_barrier((w_sent, *packed))
        w_theirs = exchange(w_sent, 0)
    with jax.named_scope("prepare"):
        mods, w, w_mine, ko, vo, ko_next, vo_next = prepare(
            slots, modulation[0], w, out_weight[0], jnp.transpose(stale_keys[0]), jnp.transpose(stale_values[0])
        )
    with jax.named_scope("first_tick"):
        places = [((0, 0, half), (1, half, rows), (2, *span), (1, 0, half)) for span in spans]
        parts = [(zero, other, own) for zero, other in zip(zeros, others, strict=True)]
        mine, theirs, olds, _ = block(*parts, places, (), mods, w, ko, vo)
        straight_a, crossing_a, straight_b, crossing_b = shift(spans, own, others, mods, mine, theirs, w_mine, w_theirs)
    with jax.named_scope("second_tick"):
        crossings = [advance(crossing, 1) for crossing in (crossing_a, crossing_b)]
        straights = [advance(straight, None) for straight in (straight_a, straight_b)]
        here = [join(crossing, straight) for crossing, straight in zip(crossings, straights, strict=True)]
        others = [exchange(rows_here, 1) for rows_here in here]
        places = [((0, half, rows), (1, half, rows), (0, 0, half), (1, 0, half))] * 2
        mine, theirs, *_ = block(here, others, places, (slots, *olds), mods, w, ko_next, vo_next)
        mine_own, mine_one = project_last(mine, theirs, w_mine, w_theirs)
        return update(here, ((0, 0, half), (1, 0, half)), mods, mine_own, exchange(mine_one, 1))[None]


def solution(mesh):
    placed = (
        P("pipe", "seq", None),
        P("pipe", None, None, "seq"),
        P("pipe", "seq", None),
        P("pipe", None, None),
        P("pipe", None, "seq"),
        P("pipe", None, "seq"),
        P("pipe", None),
    )
    return jax.shard_map(
        body, mesh=mesh, in_specs=placed, out_specs=P("pipe", "seq", None), check_vma=False
    )
```

```python
import functools
import math

import jax
import jax.numpy as jnp
from jax import lax
from jax.experimental import pallas as pl
from jax.experimental.pallas import tpu as pltpu
from jax.sharding import PartitionSpec as P

HEAD_DIM = 72
AXES = ("pipe", "seq")
VMEM_BYTES = 24 * 2**20
EXPONENT = math.log2(math.e) / math.sqrt(HEAD_DIM)


def partner(kind, section, member):
    if kind == 2:
        return member ^ 2
    if (kind + section) % 2 == 0:
        return member ^ 1
    return 3 - member


def exchange(array, kind):
    sections, members = lax.axis_size("pipe"), lax.axis_size("seq")
    moves = []
    for section in range(sections):
        for member in range(members):
            moves.append((section * members + partner(kind, section, member), section * members + member))
    return lax.ppermute(array, AXES, moves)


def advance(array, kind):
    sections, members = lax.axis_size("pipe"), lax.axis_size("seq")
    moves = []
    for section in range(sections):
        target = (section + 1) % sections
        for member in range(members):
            place = member if kind is None else partner(kind, section, member)
            moves.append((section * members + member, target * members + place))
    return lax.ppermute(array, AXES, moves)


def dot(a, b, contract_a, contract_b):
    return lax.dot_general(
        a, b, (((contract_a,), (contract_b,)), ((), ())), preferred_element_type=jnp.float32
    )


def normalize(rows, shift, scale):
    values = rows.astype(jnp.float32)
    center = jnp.mean(values, axis=-1, keepdims=True)
    values = values - center
    spread = jnp.mean(values * values, axis=-1, keepdims=True)
    return (values * lax.rsqrt(spread + 1e-06) * (1.0 + scale) + shift).astype(jnp.bfloat16)


def split_heads(source, refs):
    at = 0
    for ref in refs:
        for h in range(ref.shape[0]):
            ref[h] = source[at : at + HEAD_DIM].astype(jnp.bfloat16)
            at += HEAD_DIM


def attend(heads, jobs):
    scored = []
    for h in range(heads):
        for queries, caches, prior, store in jobs:
            q, pairs = queries(h), caches(h)
            scored.append((h, [dot(keys, q, 0, 0) for keys, _ in pairs], pairs, prior, store))
    for h, scores, pairs, prior, store in scored:
        top = functools.reduce(jnp.maximum, [jnp.max(s, 0, keepdims=True) for s in scores])
        total = out = 0.0
        if prior is not None:
            old_top, old_total, old_out = prior(h)
            top = jnp.maximum(top, old_top)
            shrink = jnp.exp2((old_top - top) * EXPONENT)
            total, out = old_total * shrink, old_out * shrink
        for s, (_, values) in zip(scores, pairs, strict=True):
            weights = jnp.exp2((s - top) * EXPONENT)
            total = total + jnp.sum(weights, 0, keepdims=True)
            out = out + dot(values, weights.astype(jnp.bfloat16), 1, 0)
        store(h, top, total, out)


def call(kernel, outs, scratch, flops, exps, operands, smem=()):
    specs = [pl.BlockSpec(memory_space=pltpu.SMEM if i in smem else pltpu.VMEM) for i in range(len(operands))]
    return pl.pallas_call(
        kernel,
        out_shape=outs,
        in_specs=specs,
        scratch_shapes=scratch,
        compiler_params=pltpu.CompilerParams(vmem_limit_bytes=VMEM_BYTES),
        cost_estimate=pl.CostEstimate(flops=flops, bytes_accessed=4 * 2**20, transcendentals=exps),
    )(*operands)


def shape(dtype, *sizes):
    return jax.ShapeDtypeStruct(sizes, dtype)


def prepare_kernel(offsets_ref, mods_ref, w_ref, wo_ref, stale_k_ref, stale_v_ref, mods_out, w_out, wo_out, *kept):
    mods_out[...] = mods_ref[...]
    w_out[...] = w_ref[...]
    wo_out[...] = wo_ref[...]
    count = kept[0].shape[2]
    for step in range(2):
        start = pl.multiple_of((1 - offsets_ref[step]) * count, count)
        for stale_ref, ref in zip((stale_k_ref, stale_v_ref), kept[2 * step : 2 * step + 2], strict=True):
            split_heads(stale_ref[:, pl.ds(start, count)].astype(jnp.float32), (ref,))


def prepare(offsets, mods, w, wo, stale_k, stale_v):
    width, context = stale_k.shape
    half = shape(jnp.bfloat16, width // HEAD_DIM, HEAD_DIM, context // 2)
    same = [shape(a.dtype, *a.shape) for a in (mods, w, wo)]
    return call(prepare_kernel, same + [half] * 4, [], 0, 0, (offsets, mods, w, wo, stale_k, stale_v), (0,))


def load_rows(refs, places, mods_ref, w_ref, normed, qkv):
    at = 0
    for i, first, last in places:
        normed[at : at + last - first] = normalize(refs[i][first:last], mods_ref[0:1], mods_ref[1:2])
        at += last - first
    qkv[...] = dot(w_ref[...], normed[...], 1, 1)


def early_kernel(places, n_parts, n_olds, *refs):
    parts, refs = refs[:n_parts], refs[n_parts:]
    olds, refs = refs[:n_olds], refs[n_olds:]
    mods_ref, w_ref, ko_ref, vo_ref, *outs, normed, qkv = refs
    q_ref, k_ref, v_ref, top_ref, total_ref, out_ref, *chosen = outs
    if olds:
        offsets_ref, *olds = olds
        for stale_ref, ref, old in zip((ko_ref, vo_ref), chosen, (olds[:2], olds[2:]), strict=True):
            ref[...] = stale_ref[...]

            @pl.when(offsets_ref[0] != offsets_ref[1])
            def _(ref=ref, old=old):
                split = old[0].shape[2]
                ref[:, :, :split] = old[0][...]
                ref[:, :, split:] = old[1][...]

        ko_ref, vo_ref = chosen
    load_rows(parts, places, mods_ref, w_ref, normed, qkv)
    split_heads(qkv, (q_ref, k_ref, v_ref))

    def store(h, top, total, out):
        top_ref[h : h + 1] = top
        total_ref[h : h + 1] = total
        out_ref[h] = out

    heads = q_ref.shape[0]
    attend(heads, [(lambda h: q_ref[h], lambda h: [(k_ref[h], v_ref[h]), (ko_ref[h], vo_ref[h])], None, store)])


def early(parts, places, olds, mods, w, ko, vo):
    rows, features = sum(last - first for _, first, last in places), w.shape[1]
    heads, _, count = ko.shape
    block = shape(jnp.bfloat16, heads, HEAD_DIM, rows)
    stat = shape(jnp.float32, 8, rows)
    chosen = [shape(jnp.bfloat16, *ko.shape)] * 2 if olds else []
    return call(
        functools.partial(early_kernel, places, len(parts), len(olds)),
        [block] * 3 + [stat, stat, shape(jnp.float32, heads, HEAD_DIM, rows)] + chosen,
        [pltpu.VMEM((rows, features), jnp.bfloat16), pltpu.VMEM((w.shape[0], rows), jnp.float32)],
        2 * rows * features * w.shape[0] + 4 * rows * (rows + count) * heads * HEAD_DIM,
        heads * rows * (rows + count), (*parts, *olds, mods, w, ko, vo), (len(parts),) if olds else (),
    )


def merge_job(mixed, at, span, early_refs, late_refs):
    q_ref, _, _, top_ref, total_ref, out_ref = early_refs
    _, kl_ref, vl_ref = late_refs
    first, last = span

    def store(h, top, total, out):
        mixed[h * HEAD_DIM : (h + 1) * HEAD_DIM, at : at + last - first] = out * (1.0 / total)

    return (
        lambda h: q_ref[h, :, first:last],
        lambda h: [(kl_ref[h], vl_ref[h])],
        lambda h: (top_ref[h : h + 1, first:last], total_ref[h : h + 1, first:last], out_ref[h, :, first:last]),
        store,
    )


def whole_job(mixed, at, span, early_refs, late_refs, ko_ref, vo_ref):
    _, k_ref, v_ref, *_ = early_refs
    ql_ref, kl_ref, vl_ref = late_refs
    first, last = span

    def store(h, top, total, out):
        mixed[h * HEAD_DIM : (h + 1) * HEAD_DIM, at : at + last - first] = out * (1.0 / total)

    return (
        lambda h: ql_ref[h, :, first:last],
        lambda h: [(k_ref[h], v_ref[h]), (ko_ref[h], vo_ref[h]), (kl_ref[h], vl_ref[h])],
        None,
        store,
    )


def finish(mixed, span, early_refs, late_refs, ko_ref, vo_ref):
    size = span[1] - span[0]
    attend(
        ko_ref.shape[0],
        [
            merge_job(mixed, 0, span, early_refs, late_refs),
            whole_job(mixed, size, span, early_refs, late_refs, ko_ref, vo_ref),
        ],
    )


def late_kernel(places, n_parts, *refs):
    parts, refs = refs[:n_parts], refs[n_parts:]
    mods_ref, w_ref, ko_ref, vo_ref, *early_refs = refs[:10]
    sent_ref, *late_refs, normed, qkv, mixed = refs[10:]
    load_rows(parts, places, mods_ref, w_ref, normed, qkv)
    split_heads(qkv, late_refs)
    finish(mixed, (0, mixed.shape[1] // 2), early_refs, late_refs, ko_ref, vo_ref)
    sent_ref[...] = mixed[...].astype(jnp.bfloat16)


def late(parts, places, mods, w, ko, vo, early_state):
    rows, features = sum(last - first for _, first, last in places), w.shape[1]
    heads, _, count = ko.shape
    width = heads * HEAD_DIM
    return call(
        functools.partial(late_kernel, places, len(parts)),
        [shape(jnp.bfloat16, width, rows)] + [shape(jnp.bfloat16, heads, HEAD_DIM, rows)] * 3,
        [
            pltpu.VMEM((rows, features), jnp.bfloat16),
            pltpu.VMEM((w.shape[0], rows), jnp.float32),
            pltpu.VMEM((width, rows), jnp.float32),
        ],
        2 * rows * features * w.shape[0] + 4 * rows * count * width,
        heads * rows * count, (*parts, mods, w, ko, vo, *early_state),
    )


def rest_kernel(ko_ref, vo_ref, *refs):
    early_refs, late_refs, (kept_ref, mixed) = refs[:6], refs[6:9], refs[9:]
    columns = mixed.shape[1]
    finish(mixed, (columns // 2, columns), early_refs, late_refs, ko_ref, vo_ref)
    kept_ref[...] = mixed[...].astype(jnp.bfloat16)


def rest(ko, vo, early_state, late_state):
    heads, _, count = ko.shape
    width, rows = heads * HEAD_DIM, late_state[0].shape[2]
    return call(
        rest_kernel, shape(jnp.bfloat16, width, rows), [pltpu.VMEM((width, rows), jnp.float32)],
        64 * 4 * rows * count * width, heads * rows * count, (ko, vo, *early_state, *late_state),
    )


def block(early_parts, late_parts, places, olds, mods, w, ko, vo, also=()):
    state = early(early_parts, places[0], olds, mods, w, ko, vo)
    if olds:
        *state, ko, vo = state
    sent, *late_state = late(late_parts, places[1], mods, w, ko, vo, state)
    theirs = exchange(sent, 0)
    mine = rest(ko, vo, state, late_state)
    return mine, theirs, (state[1], late_state[1], state[2], late_state[2]), also


def both_sums(mine_ref, theirs_ref, w_mine_ref, w_theirs_ref):
    return dot(mine_ref[...], w_mine_ref[...], 0, 0) + dot(theirs_ref[...], w_theirs_ref[...], 0, 0)


def shift_kernel(spans, own_ref, other_a, other_b, mods_ref, *refs):
    *refs, straight_a, crossing_a, straight_b, crossing_b = refs
    half = straight_a.shape[0] // 2
    added = mods_ref[2:3] * both_sums(*refs)
    chunks = ((other_a, straight_a, crossing_a), (other_b, straight_b, crossing_b))
    for i, ((first, last), (other, straight, crossing)) in enumerate(zip(spans, chunks, strict=True)):
        at = 2 * i * half
        own, one = added[at : at + half], added[at + half : at + 2 * half]
        straight[:half] = (own_ref[first:last].astype(jnp.float32) + own).astype(jnp.bfloat16)
        straight[half:] = (other[:half].astype(jnp.float32) + one).astype(jnp.bfloat16)
        crossing[:half] = one.astype(jnp.bfloat16)
        crossing[half:] = own.astype(jnp.bfloat16)


def shift(spans, own, others, mods, mine, theirs, w_mine, w_theirs):
    rows, features, width = mine.shape[1], w_mine.shape[1], mine.shape[0]
    return call(
        functools.partial(shift_kernel, spans), [shape(jnp.bfloat16, rows // 2, features)] * 4, [],
        4 * rows * features * width, 0, (own, *others, mods, mine, theirs, w_mine, w_theirs),
    )


def join_kernel(crossing_ref, straight_ref, out_ref):
    total = straight_ref[...].astype(jnp.float32) + crossing_ref[...].astype(jnp.float32)
    out_ref[...] = total.astype(jnp.bfloat16)


def join(crossing, straight):
    return call(join_kernel, shape(straight.dtype, *straight.shape), [], straight.size, 0, (crossing, straight))


def last_kernel(*refs):
    *refs, kept_ref, sent_ref = refs
    rows = kept_ref.shape[0]
    total = both_sums(*refs)
    kept_ref[...] = total[:rows]
    sent_ref[...] = total[rows:].astype(jnp.bfloat16)


def project_last(mine, theirs, w_mine, w_theirs):
    rows, features, width = mine.shape[1] // 2, w_mine.shape[1], mine.shape[0]
    return call(
        last_kernel, [shape(jnp.float32, rows, features), shape(jnp.bfloat16, rows, features)], [],
        8 * rows * features * width, 0, (mine, theirs, w_mine, w_theirs),
    )


def update_kernel(places, n_parts, mods_ref, *refs):
    parts, (mine_ref, theirs_ref, out_ref) = refs[:n_parts], refs[n_parts:]
    attended = mine_ref[...].astype(jnp.float32) + theirs_ref[...].astype(jnp.float32)
    at = 0
    for i, first, last in places:
        here = slice(at, at + last - first)
        new = parts[i][first:last].astype(jnp.float32) + mods_ref[2:3] * attended[here]
        out_ref[here] = new.astype(jnp.bfloat16)
        at += last - first


def update(parts, places, mods, mine, theirs):
    return call(
        functools.partial(update_kernel, places, len(parts)),
        shape(jnp.bfloat16, *mine.shape), [], 4 * mine.size, 0, (mods, *parts, mine, theirs),
    )


def pack_kernel(first, last, own_ref, zero_ref, out_ref):
    half = last - first
    out_ref[:half] = own_ref[first:last]
    out_ref[half:] = zero_ref[...]


def pack(own, first, last, zero):
    return call(
        functools.partial(pack_kernel, first, last),
        shape(own.dtype, 2 * (last - first), own.shape[1]), [], 0, 0, (own, zero),
    )


def body(patches, qkv_weight, out_weight, modulation, stale_keys, stale_values, offsets):
    width = qkv_weight.shape[3]
    features = qkv_weight.shape[1]
    w = jnp.transpose(qkv_weight[0], (1, 2, 0)).reshape(3 * width, features)
    w_sent = out_weight[0]
    slots = offsets[0]
    own = patches[0]
    rows = own.shape[0]
    half = rows // 2
    spans = ((0, half), (half, rows))

    with jax.named_scope("first_gather"):
        zeros = [exchange(own[first:last], 0) for first, last in spans]
        packed = [pack(own, *span, zero) for span, zero in zip(spans, zeros, strict=True)]
        others = [exchange(rows_here, 1) for rows_here in packed]
        w_sent, *_ = lax.optimization_barrier((w_sent, *packed))
        w_theirs = exchange(w_sent, 0)
    with jax.named_scope("prepare"):
        mods, w, w_mine, ko, vo, ko_next, vo_next = prepare(
            slots, modulation[0], w, out_weight[0], jnp.transpose(stale_keys[0]), jnp.transpose(stale_values[0])
        )
    with jax.named_scope("first_tick"):
        places = [((0, 0, half), (1, half, rows), (2, *span), (1, 0, half)) for span in spans]
        parts = [(zero, other, own) for zero, other in zip(zeros, others, strict=True)]
        mine, theirs, olds, _ = block(*parts, places, (), mods, w, ko, vo)
        straight_a, crossing_a, straight_b, crossing_b = shift(spans, own, others, mods, mine, theirs, w_mine, w_theirs)
    with jax.named_scope("second_tick"):
        straights = [advance(straight, None) for straight in (straight_a, straight_b)]
        crossings = [advance(crossing, 1) for crossing in (crossing_a, crossing_b)]
        here = [join(straight, crossing) for crossing, straight in zip(crossings, straights, strict=True)]
        others = [exchange(rows_here, 1) for rows_here in here]
        places = [((0, half, rows), (1, half, rows), (0, 0, half), (1, 0, half))] * 2
        mine, theirs, *_ = block(here, others, places, (slots, *olds), mods, w, ko_next, vo_next)
        mine_own, mine_one = project_last(mine, theirs, w_mine, w_theirs)
        return update(here, ((0, 0, half), (1, 0, half)), mods, mine_own, exchange(mine_one, 1))[None]


def solution(mesh):
    placed = (
        P("pipe", "seq", None),
        P("pipe", None, None, "seq"),
        P("pipe", "seq", None),
        P("pipe", None, None),
        P("pipe", None, "seq"),
        P("pipe", None, "seq"),
        P("pipe", None),
    )
    return jax.shard_map(
        body, mesh=mesh, in_specs=placed, out_specs=P("pipe", "seq", None), check_vma=False
    )
```

```python
import functools
import math

import jax
import jax.numpy as jnp
from jax import lax
from jax.experimental import pallas as pl
from jax.experimental.pallas import tpu as pltpu
from jax.sharding import PartitionSpec as P

HEAD_DIM = 72
AXES = ("pipe", "seq")
VMEM_BYTES = 24 * 2**20
EXPONENT = math.log2(math.e) / math.sqrt(HEAD_DIM)


def partner(kind, section, member):
    if kind == 2:
        return member ^ 2
    if (kind + section) % 2 == 0:
        return member ^ 1
    return 3 - member


def exchange(array, kind):
    sections, members = lax.axis_size("pipe"), lax.axis_size("seq")
    moves = []
    for section in range(sections):
        for member in range(members):
            moves.append((section * members + partner(kind, section, member), section * members + member))
    return lax.ppermute(array, AXES, moves)


def advance(array, kind):
    sections, members = lax.axis_size("pipe"), lax.axis_size("seq")
    moves = []
    for section in range(sections):
        target = (section + 1) % sections
        for member in range(members):
            place = member if kind is None else partner(kind, section, member)
            moves.append((section * members + member, target * members + place))
    return lax.ppermute(array, AXES, moves)


def dot(a, b, contract_a, contract_b):
    return lax.dot_general(
        a, b, (((contract_a,), (contract_b,)), ((), ())), preferred_element_type=jnp.float32
    )


def normalize(rows, shift, scale):
    values = rows.astype(jnp.float32)
    center = jnp.mean(values, axis=-1, keepdims=True)
    values = values - center
    spread = jnp.mean(values * values, axis=-1, keepdims=True)
    return (values * lax.rsqrt(spread + 1e-06) * (1.0 + scale) + shift).astype(jnp.bfloat16)


def split_heads(source, refs):
    at = 0
    for ref in refs:
        for h in range(ref.shape[0]):
            ref[h] = source[at : at + HEAD_DIM].astype(jnp.bfloat16)
            at += HEAD_DIM


def attend(heads, jobs):
    scored = []
    for h in range(heads):
        for queries, caches, prior, store in jobs:
            q, pairs = queries(h), caches(h)
            scored.append((h, [dot(keys, q, 0, 0) for keys, _ in pairs], pairs, prior, store))
    for h, scores, pairs, prior, store in scored:
        top = functools.reduce(jnp.maximum, [jnp.max(s, 0, keepdims=True) for s in scores])
        total = out = 0.0
        if prior is not None:
            old_top, old_total, old_out = prior(h)
            top = jnp.maximum(top, old_top)
            shrink = jnp.exp2((old_top - top) * EXPONENT)
            total, out = old_total * shrink, old_out * shrink
        for s, (_, values) in zip(scores, pairs, strict=True):
            weights = jnp.exp2((s - top) * EXPONENT)
            total = total + jnp.sum(weights, 0, keepdims=True)
            out = out + dot(values, weights.astype(jnp.bfloat16), 1, 0)
        store(h, top, total, out)


def call(kernel, outs, scratch, flops, exps, operands, smem=()):
    specs = [pl.BlockSpec(memory_space=pltpu.SMEM if i in smem else pltpu.VMEM) for i in range(len(operands))]
    return pl.pallas_call(
        kernel,
        out_shape=outs,
        in_specs=specs,
        scratch_shapes=scratch,
        compiler_params=pltpu.CompilerParams(vmem_limit_bytes=VMEM_BYTES),
        cost_estimate=pl.CostEstimate(flops=flops, bytes_accessed=4 * 2**20, transcendentals=exps),
    )(*operands)


def shape(dtype, *sizes):
    return jax.ShapeDtypeStruct(sizes, dtype)


def prepare_kernel(offsets_ref, mods_ref, w_ref, wo_ref, stale_k_ref, stale_v_ref, mods_out, w_out, wo_out, *kept):
    mods_out[...] = mods_ref[...]
    w_out[...] = w_ref[...]
    wo_out[...] = wo_ref[...]
    count = kept[0].shape[2]
    for step in range(2):
        start = pl.multiple_of((1 - offsets_ref[step]) * count, count)
        for stale_ref, ref in zip((stale_k_ref, stale_v_ref), kept[2 * step : 2 * step + 2], strict=True):
            split_heads(stale_ref[:, pl.ds(start, count)].astype(jnp.float32), (ref,))


def prepare(offsets, mods, w, wo, stale_k, stale_v):
    width, context = stale_k.shape
    half = shape(jnp.bfloat16, width // HEAD_DIM, HEAD_DIM, context // 2)
    same = [shape(a.dtype, *a.shape) for a in (mods, w, wo)]
    return call(prepare_kernel, same + [half] * 4, [], 0, 0, (offsets, mods, w, wo, stale_k, stale_v), (0,))


def load_rows(refs, places, mods_ref, w_ref, normed, qkv):
    at = 0
    for i, first, last in places:
        normed[at : at + last - first] = normalize(refs[i][first:last], mods_ref[0:1], mods_ref[1:2])
        at += last - first
    qkv[...] = dot(w_ref[...], normed[...], 1, 1)


def early_kernel(places, n_parts, n_olds, *refs):
    parts, refs = refs[:n_parts], refs[n_parts:]
    olds, refs = refs[:n_olds], refs[n_olds:]
    mods_ref, w_ref, ko_ref, vo_ref, *outs, normed, qkv = refs
    q_ref, k_ref, v_ref, top_ref, total_ref, out_ref, *chosen = outs
    if olds:
        offsets_ref, *olds = olds
        for stale_ref, ref, old in zip((ko_ref, vo_ref), chosen, (olds[:2], olds[2:]), strict=True):
            ref[...] = stale_ref[...]

            @pl.when(offsets_ref[0] != offsets_ref[1])
            def _(ref=ref, old=old):
                split = old[0].shape[2]
                ref[:, :, :split] = old[0][...]
                ref[:, :, split:] = old[1][...]

        ko_ref, vo_ref = chosen
    load_rows(parts, places, mods_ref, w_ref, normed, qkv)
    split_heads(qkv, (q_ref, k_ref, v_ref))

    def store(h, top, total, out):
        top_ref[h : h + 1] = top
        total_ref[h : h + 1] = total
        out_ref[h] = out

    heads = q_ref.shape[0]
    attend(heads, [(lambda h: q_ref[h], lambda h: [(k_ref[h], v_ref[h]), (ko_ref[h], vo_ref[h])], None, store)])


def early(parts, places, olds, mods, w, ko, vo):
    rows, features = sum(last - first for _, first, last in places), w.shape[1]
    heads, _, count = ko.shape
    block = shape(jnp.bfloat16, heads, HEAD_DIM, rows)
    stat = shape(jnp.float32, 8, rows)
    chosen = [shape(jnp.bfloat16, *ko.shape)] * 2 if olds else []
    return call(
        functools.partial(early_kernel, places, len(parts), len(olds)),
        [block] * 3 + [stat, stat, shape(jnp.float32, heads, HEAD_DIM, rows)] + chosen,
        [pltpu.VMEM((rows, features), jnp.bfloat16), pltpu.VMEM((w.shape[0], rows), jnp.float32)],
        2 * rows * features * w.shape[0] + 4 * rows * (rows + count) * heads * HEAD_DIM,
        heads * rows * (rows + count), (*parts, *olds, mods, w, ko, vo), (len(parts),) if olds else (),
    )


def merge_job(mixed, at, span, early_refs, late_refs):
    q_ref, _, _, top_ref, total_ref, out_ref = early_refs
    _, kl_ref, vl_ref = late_refs
    first, last = span

    def store(h, top, total, out):
        mixed[h * HEAD_DIM : (h + 1) * HEAD_DIM, at : at + last - first] = out * (1.0 / total)

    return (
        lambda h: q_ref[h, :, first:last],
        lambda h: [(kl_ref[h], vl_ref[h])],
        lambda h: (top_ref[h : h + 1, first:last], total_ref[h : h + 1, first:last], out_ref[h, :, first:last]),
        store,
    )


def whole_job(mixed, at, span, early_refs, late_refs, ko_ref, vo_ref):
    _, k_ref, v_ref, *_ = early_refs
    ql_ref, kl_ref, vl_ref = late_refs
    first, last = span

    def store(h, top, total, out):
        mixed[h * HEAD_DIM : (h + 1) * HEAD_DIM, at : at + last - first] = out * (1.0 / total)

    return (
        lambda h: ql_ref[h, :, first:last],
        lambda h: [(k_ref[h], v_ref[h]), (ko_ref[h], vo_ref[h]), (kl_ref[h], vl_ref[h])],
        None,
        store,
    )


def finish(mixed, span, early_refs, late_refs, ko_ref, vo_ref):
    size = span[1] - span[0]
    attend(
        ko_ref.shape[0],
        [
            merge_job(mixed, 0, span, early_refs, late_refs),
            whole_job(mixed, size, span, early_refs, late_refs, ko_ref, vo_ref),
        ],
    )


def late_kernel(places, n_parts, *refs):
    parts, refs = refs[:n_parts], refs[n_parts:]
    mods_ref, w_ref, ko_ref, vo_ref, *early_refs = refs[:10]
    sent_ref, *late_refs, normed, qkv, mixed = refs[10:]
    load_rows(parts, places, mods_ref, w_ref, normed, qkv)
    split_heads(qkv, late_refs)
    finish(mixed, (0, mixed.shape[1] // 2), early_refs, late_refs, ko_ref, vo_ref)
    sent_ref[...] = mixed[...].astype(jnp.bfloat16)


def late(parts, places, mods, w, ko, vo, early_state):
    rows, features = sum(last - first for _, first, last in places), w.shape[1]
    heads, _, count = ko.shape
    width = heads * HEAD_DIM
    return call(
        functools.partial(late_kernel, places, len(parts)),
        [shape(jnp.bfloat16, width, rows)] + [shape(jnp.bfloat16, heads, HEAD_DIM, rows)] * 3,
        [
            pltpu.VMEM((rows, features), jnp.bfloat16),
            pltpu.VMEM((w.shape[0], rows), jnp.float32),
            pltpu.VMEM((width, rows), jnp.float32),
        ],
        2 * rows * features * w.shape[0] + 4 * rows * count * width,
        heads * rows * count, (*parts, mods, w, ko, vo, *early_state),
    )


def rest_kernel(ko_ref, vo_ref, *refs):
    early_refs, late_refs, (kept_ref, mixed) = refs[:6], refs[6:9], refs[9:]
    columns = mixed.shape[1]
    finish(mixed, (columns // 2, columns), early_refs, late_refs, ko_ref, vo_ref)
    kept_ref[...] = mixed[...].astype(jnp.bfloat16)


def rest(ko, vo, early_state, late_state):
    heads, _, count = ko.shape
    width, rows = heads * HEAD_DIM, late_state[0].shape[2]
    return call(
        rest_kernel, shape(jnp.bfloat16, width, rows), [pltpu.VMEM((width, rows), jnp.float32)],
        64 * 4 * rows * count * width, heads * rows * count, (ko, vo, *early_state, *late_state),
    )


def block(early_parts, late_parts, places, olds, mods, w, ko, vo, also=()):
    state = early(early_parts, places[0], olds, mods, w, ko, vo)
    if olds:
        *state, ko, vo = state
    sent, *late_state = late(late_parts, places[1], mods, w, ko, vo, state)
    theirs = exchange(sent, 0)
    mine = rest(ko, vo, state, late_state)
    return mine, theirs, (state[1], late_state[1], state[2], late_state[2]), also


def both_sums(first, last, mine_ref, theirs_ref, w_mine_ref, w_theirs_ref):
    mine, theirs = (ref[:, first:last] for ref in (mine_ref, theirs_ref))
    return dot(mine, w_mine_ref[...], 0, 0) + dot(theirs, w_theirs_ref[...], 0, 0)


def shift_kernel(chunk, own_ref, other_ref, mods_ref, *refs):
    *refs, straight_ref, crossing_ref = refs
    half = own_ref.shape[0]
    added = mods_ref[2:3] * both_sums(2 * chunk * half, (2 * chunk + 2) * half, *refs)
    straight_ref[:half] = (own_ref[...].astype(jnp.float32) + added[:half]).astype(jnp.bfloat16)
    straight_ref[half:] = (other_ref[:half].astype(jnp.float32) + added[half:]).astype(jnp.bfloat16)
    crossing_ref[:half] = added[half:].astype(jnp.bfloat16)
    crossing_ref[half:] = added[:half].astype(jnp.bfloat16)


def shift(chunk, own, other, mods, mine, theirs, w_mine, w_theirs):
    rows, features, width = 2 * own.shape[0], w_mine.shape[1], mine.shape[0]
    return call(
        functools.partial(shift_kernel, chunk), [shape(jnp.bfloat16, rows, features)] * 2, [],
        4 * rows * features * width, 0, (own, other, mods, mine, theirs, w_mine, w_theirs),
    )


def join_kernel(straight_ref, crossing_ref, out_ref):
    total = straight_ref[...].astype(jnp.float32) + crossing_ref[...].astype(jnp.float32)
    out_ref[...] = total.astype(jnp.bfloat16)


def join(straight, crossing):
    return call(join_kernel, shape(straight.dtype, *straight.shape), [], straight.size, 0, (straight, crossing))


def part_kernel(first, *refs):
    *refs, out_ref = refs
    out_ref[...] = both_sums(first, first + out_ref.shape[0], *refs).astype(out_ref.dtype)


def part(first, dtype, mine, theirs, w_mine, w_theirs):
    rows, features, width = mine.shape[1] // 2, w_mine.shape[1], mine.shape[0]
    return call(
        functools.partial(part_kernel, first), shape(dtype, rows, features), [],
        4 * rows * features * width, 0, (mine, theirs, w_mine, w_theirs),
    )


def update_kernel(places, n_parts, mods_ref, *refs):
    parts, (mine_ref, theirs_ref, out_ref) = refs[:n_parts], refs[n_parts:]
    attended = mine_ref[...].astype(jnp.float32) + theirs_ref[...].astype(jnp.float32)
    at = 0
    for i, first, last in places:
        here = slice(at, at + last - first)
        new = parts[i][first:last].astype(jnp.float32) + mods_ref[2:3] * attended[here]
        out_ref[here] = new.astype(jnp.bfloat16)
        at += last - first


def update(parts, places, mods, mine, theirs):
    return call(
        functools.partial(update_kernel, places, len(parts)),
        shape(jnp.bfloat16, *mine.shape), [], 4 * mine.size, 0, (mods, *parts, mine, theirs),
    )


def halve_kernel(own_ref, a_ref, b_ref):
    half = a_ref.shape[0]
    a_ref[...] = own_ref[:half]
    b_ref[...] = own_ref[half:]


def halve(own):
    rows, features = own.shape
    return call(halve_kernel, [shape(own.dtype, rows // 2, features)] * 2, [], 0, 0, (own,))


def pack_kernel(first, own_ref, zero_ref, out_ref):
    half = own_ref.shape[0]
    out_ref[:half] = own_ref[...]
    out_ref[half:] = zero_ref[first : first + half]


def pack(own, first, zero):
    rows, features = own.shape
    return call(
        functools.partial(pack_kernel, first), shape(own.dtype, 2 * rows, features), [], 0, 0, (own, zero)
    )


def body(patches, qkv_weight, out_weight, modulation, stale_keys, stale_values, offsets):
    width = qkv_weight.shape[3]
    features = qkv_weight.shape[1]
    w = jnp.transpose(qkv_weight[0], (1, 2, 0)).reshape(3 * width, features)
    w_sent = out_weight[0]
    slots = offsets[0]
    own = patches[0]
    rows = own.shape[0]
    half = rows // 2
    spans = ((0, half), (half, rows))

    with jax.named_scope("first_gather"):
        zero = exchange(own, 0)
        owns = halve(own)
        packed = [pack(own_half, first, zero) for own_half, (first, _) in zip(owns, spans, strict=True)]
        others = [exchange(rows_here, 1) for rows_here in packed]
        w_sent, *_ = lax.optimization_barrier((w_sent, *packed))
        w_theirs = exchange(w_sent, 0)
    with jax.named_scope("prepare"):
        mods, w, w_mine, ko, vo, ko_next, vo_next = prepare(
            slots, modulation[0], w, out_weight[0], jnp.transpose(stale_keys[0]), jnp.transpose(stale_values[0])
        )
    with jax.named_scope("first_tick"):
        places = [((0, *span), (1, half, rows), (2, 0, half), (1, 0, half)) for span in spans]
        parts = [(zero, other, own_half) for other, own_half in zip(others, owns, strict=True)]
        mine, theirs, olds, _ = block(*parts, places, (), mods, w, ko, vo)
        shifted = [
            shift(i, own_half, other, mods, mine, theirs, w_mine, w_theirs)
            for i, (own_half, other) in enumerate(zip(owns, others, strict=True))
        ]
    with jax.named_scope("second_tick"):
        straights = [advance(straight, None) for straight, _ in shifted]
        crossings = [advance(crossing, 1) for _, crossing in shifted]
        here = [join(straight, crossing) for straight, crossing in zip(straights, crossings, strict=True)]
        others = [exchange(rows_here, 1) for rows_here in here]
        places = [((0, half, rows), (1, half, rows), (0, 0, half), (1, 0, half))] * 2
        mine, theirs, *_ = block(here, others, places, (slots, *olds), mods, w, ko_next, vo_next)
        from_one = exchange(part(rows, jnp.bfloat16, mine, theirs, w_mine, w_theirs), 1)
        mine_own = part(0, jnp.float32, mine, theirs, w_mine, w_theirs)
        return update(here, ((0, 0, half), (1, 0, half)), mods, mine_own, from_one)[None]


def solution(mesh):
    placed = (
        P("pipe", "seq", None),
        P("pipe", None, None, "seq"),
        P("pipe", "seq", None),
        P("pipe", None, None),
        P("pipe", None, "seq"),
        P("pipe", None, "seq"),
        P("pipe", None),
    )
    return jax.shard_map(
        body, mesh=mesh, in_specs=placed, out_specs=P("pipe", "seq", None), check_vma=False
    )
```

```python
import functools
import math

import jax
import jax.numpy as jnp
from jax import lax
from jax.experimental import pallas as pl
from jax.experimental.pallas import tpu as pltpu
from jax.sharding import PartitionSpec as P

HEAD_DIM = 72
AXES = ("pipe", "seq")
SMALL_CHUNK = 6
VMEM_BYTES = 24 * 2**20
EXPONENT = math.log2(math.e) / math.sqrt(HEAD_DIM)


def partner(kind, section, member):
    if kind == 2:
        return member ^ 2
    if (kind + section) % 2 == 0:
        return member ^ 1
    return 3 - member


def exchange(array, kind):
    sections, members = lax.axis_size("pipe"), lax.axis_size("seq")
    moves = []
    for section in range(sections):
        for member in range(members):
            moves.append((section * members + partner(kind, section, member), section * members + member))
    return lax.ppermute(array, AXES, moves)


def advance(array, kind):
    sections, members = lax.axis_size("pipe"), lax.axis_size("seq")
    moves = []
    for section in range(sections):
        target = (section + 1) % sections
        for member in range(members):
            place = member if kind is None else partner(kind, section, member)
            moves.append((section * members + member, target * members + place))
    return lax.ppermute(array, AXES, moves)


def dot(a, b, contract_a, contract_b):
    return lax.dot_general(
        a, b, (((contract_a,), (contract_b,)), ((), ())), preferred_element_type=jnp.float32
    )


def normalize(rows, shift, scale):
    values = rows.astype(jnp.float32)
    center = jnp.mean(values, axis=-1, keepdims=True)
    values = values - center
    spread = jnp.mean(values * values, axis=-1, keepdims=True)
    return (values * lax.rsqrt(spread + 1e-06) * (1.0 + scale) + shift).astype(jnp.bfloat16)


def split_heads(source, refs):
    at = 0
    for ref in refs:
        for h in range(ref.shape[0]):
            ref[h] = source[at : at + HEAD_DIM].astype(jnp.bfloat16)
            at += HEAD_DIM


def attend(heads, jobs):
    scored = []
    for h in range(heads):
        for queries, caches, prior, store in jobs:
            q, pairs = queries(h), caches(h)
            scored.append((h, [dot(keys, q, 0, 0) for keys, _ in pairs], pairs, prior, store))
    for h, scores, pairs, prior, store in scored:
        top = functools.reduce(jnp.maximum, [jnp.max(s, 0, keepdims=True) for s in scores])
        total = out = 0.0
        if prior is not None:
            old_top, old_total, old_out = prior(h)
            top = jnp.maximum(top, old_top)
            shrink = jnp.exp2((old_top - top) * EXPONENT)
            total, out = old_total * shrink, old_out * shrink
        for s, (_, values) in zip(scores, pairs, strict=True):
            weights = jnp.exp2((s - top) * EXPONENT)
            total = total + jnp.sum(weights, 0, keepdims=True)
            out = out + dot(values, weights.astype(jnp.bfloat16), 1, 0)
        store(h, top, total, out)


def call(kernel, outs, scratch, flops, exps, operands, smem=()):
    specs = [pl.BlockSpec(memory_space=pltpu.SMEM if i in smem else pltpu.VMEM) for i in range(len(operands))]
    return pl.pallas_call(
        kernel,
        out_shape=outs,
        in_specs=specs,
        scratch_shapes=scratch,
        compiler_params=pltpu.CompilerParams(vmem_limit_bytes=VMEM_BYTES),
        cost_estimate=pl.CostEstimate(flops=flops, bytes_accessed=4 * 2**20, transcendentals=exps),
    )(*operands)


def shape(dtype, *sizes):
    return jax.ShapeDtypeStruct(sizes, dtype)


def prepare_kernel(offsets_ref, mods_ref, w_ref, wo_ref, stale_k_ref, stale_v_ref, mods_out, w_out, wo_out, *kept):
    mods_out[...] = mods_ref[...]
    w_out[...] = w_ref[...]
    wo_out[...] = wo_ref[...]
    count = kept[0].shape[2]
    for step in range(2):
        start = pl.multiple_of((1 - offsets_ref[step]) * count, count)
        for stale_ref, ref in zip((stale_k_ref, stale_v_ref), kept[2 * step : 2 * step + 2], strict=True):
            split_heads(stale_ref[:, pl.ds(start, count)].astype(jnp.float32), (ref,))


def prepare(offsets, mods, w, wo, stale_k, stale_v):
    width, context = stale_k.shape
    half = shape(jnp.bfloat16, width // HEAD_DIM, HEAD_DIM, context // 2)
    same = [shape(a.dtype, *a.shape) for a in (mods, w, wo)]
    return call(prepare_kernel, same + [half] * 4, [], 0, 0, (offsets, mods, w, wo, stale_k, stale_v), (0,))


def load_rows(refs, places, mods_ref, w_ref, normed, qkv):
    at = 0
    for i, first, last in places:
        normed[at : at + last - first] = normalize(refs[i][first:last], mods_ref[0:1], mods_ref[1:2])
        at += last - first
    qkv[...] = dot(w_ref[...], normed[...], 1, 1)


def early_kernel(places, n_parts, n_olds, *refs):
    parts, refs = refs[:n_parts], refs[n_parts:]
    olds, refs = refs[:n_olds], refs[n_olds:]
    mods_ref, w_ref, ko_ref, vo_ref, *outs, normed, qkv = refs
    q_ref, k_ref, v_ref, top_ref, total_ref, out_ref, *chosen = outs
    if olds:
        offsets_ref, *olds = olds
        for stale_ref, ref, old in zip((ko_ref, vo_ref), chosen, (olds[:2], olds[2:]), strict=True):
            ref[...] = stale_ref[...]

            @pl.when(offsets_ref[0] != offsets_ref[1])
            def _(ref=ref, old=old):
                split = old[0].shape[2]
                ref[:, :, :split] = old[0][...]
                ref[:, :, split:] = old[1][...]

        ko_ref, vo_ref = chosen
    load_rows(parts, places, mods_ref, w_ref, normed, qkv)
    split_heads(qkv, (q_ref, k_ref, v_ref))

    def store(h, top, total, out):
        top_ref[h : h + 1] = top
        total_ref[h : h + 1] = total
        out_ref[h] = out

    heads = q_ref.shape[0]
    attend(heads, [(lambda h: q_ref[h], lambda h: [(k_ref[h], v_ref[h]), (ko_ref[h], vo_ref[h])], None, store)])


def early(parts, places, olds, mods, w, ko, vo):
    rows, features = sum(last - first for _, first, last in places), w.shape[1]
    heads, _, count = ko.shape
    block = shape(jnp.bfloat16, heads, HEAD_DIM, rows)
    stat = shape(jnp.float32, 8, rows)
    chosen = [shape(jnp.bfloat16, *ko.shape)] * 2 if olds else []
    return call(
        functools.partial(early_kernel, places, len(parts), len(olds)),
        [block] * 3 + [stat, stat, shape(jnp.float32, heads, HEAD_DIM, rows)] + chosen,
        [pltpu.VMEM((rows, features), jnp.bfloat16), pltpu.VMEM((w.shape[0], rows), jnp.float32)],
        2 * rows * features * w.shape[0] + 4 * rows * (rows + count) * heads * HEAD_DIM,
        heads * rows * (rows + count), (*parts, *olds, mods, w, ko, vo), (len(parts),) if olds else (),
    )


def merge_job(mixed, at, span, early_refs, late_refs):
    q_ref, _, _, top_ref, total_ref, out_ref = early_refs
    _, kl_ref, vl_ref = late_refs
    first, last = span

    def store(h, top, total, out):
        mixed[h * HEAD_DIM : (h + 1) * HEAD_DIM, at : at + last - first] = out * (1.0 / total)

    return (
        lambda h: q_ref[h, :, first:last],
        lambda h: [(kl_ref[h], vl_ref[h])],
        lambda h: (top_ref[h : h + 1, first:last], total_ref[h : h + 1, first:last], out_ref[h, :, first:last]),
        store,
    )


def whole_job(mixed, at, span, early_refs, late_refs, ko_ref, vo_ref):
    _, k_ref, v_ref, *_ = early_refs
    ql_ref, kl_ref, vl_ref = late_refs
    first, last = span

    def store(h, top, total, out):
        mixed[h * HEAD_DIM : (h + 1) * HEAD_DIM, at : at + last - first] = out * (1.0 / total)

    return (
        lambda h: ql_ref[h, :, first:last],
        lambda h: [(k_ref[h], v_ref[h]), (ko_ref[h], vo_ref[h]), (kl_ref[h], vl_ref[h])],
        None,
        store,
    )


def finish(mixed, span, early_refs, late_refs, ko_ref, vo_ref):
    size = span[1] - span[0]
    attend(
        ko_ref.shape[0],
        [
            merge_job(mixed, 0, span, early_refs, late_refs),
            whole_job(mixed, size, span, early_refs, late_refs, ko_ref, vo_ref),
        ],
    )


def late_kernel(places, n_parts, *refs):
    parts, refs = refs[:n_parts], refs[n_parts:]
    mods_ref, w_ref, ko_ref, vo_ref, *early_refs = refs[:10]
    sent_ref, *late_refs, normed, qkv, mixed = refs[10:]
    load_rows(parts, places, mods_ref, w_ref, normed, qkv)
    split_heads(qkv, late_refs)
    finish(mixed, (0, mixed.shape[1] // 2), early_refs, late_refs, ko_ref, vo_ref)
    sent_ref[...] = mixed[...].astype(jnp.bfloat16)


def late(parts, places, mods, w, ko, vo, early_state):
    rows, features = sum(last - first for _, first, last in places), w.shape[1]
    heads, _, count = ko.shape
    width = heads * HEAD_DIM
    return call(
        functools.partial(late_kernel, places, len(parts)),
        [shape(jnp.bfloat16, width, rows)] + [shape(jnp.bfloat16, heads, HEAD_DIM, rows)] * 3,
        [
            pltpu.VMEM((rows, features), jnp.bfloat16),
            pltpu.VMEM((w.shape[0], rows), jnp.float32),
            pltpu.VMEM((width, rows), jnp.float32),
        ],
        2 * rows * features * w.shape[0] + 4 * rows * count * width,
        heads * rows * count, (*parts, mods, w, ko, vo, *early_state),
    )


def rest_kernel(ko_ref, vo_ref, *refs):
    early_refs, late_refs, (kept_ref, mixed) = refs[:6], refs[6:9], refs[9:]
    columns = mixed.shape[1]
    finish(mixed, (columns // 2, columns), early_refs, late_refs, ko_ref, vo_ref)
    kept_ref[...] = mixed[...].astype(jnp.bfloat16)


def rest(ko, vo, early_state, late_state):
    heads, _, count = ko.shape
    width, rows = heads * HEAD_DIM, late_state[0].shape[2]
    return call(
        rest_kernel, shape(jnp.bfloat16, width, rows), [pltpu.VMEM((width, rows), jnp.float32)],
        64 * 4 * rows * count * width, heads * rows * count, (ko, vo, *early_state, *late_state),
    )


def block(early_parts, late_parts, places, olds, mods, w, ko, vo, also=()):
    state = early(early_parts, places[0], olds, mods, w, ko, vo)
    if olds:
        *state, ko, vo = state
    sent, *late_state = late(late_parts, places[1], mods, w, ko, vo, state)
    theirs = exchange(sent, 0)
    mine = rest(ko, vo, state, late_state)
    return mine, theirs, (state[1], late_state[1], state[2], late_state[2]), also


def both_sums(first, last, mine_ref, theirs_ref, w_mine_ref, w_theirs_ref):
    mine, theirs = (ref[:, first:last] for ref in (mine_ref, theirs_ref))
    return dot(mine, w_mine_ref[...], 0, 0) + dot(theirs, w_theirs_ref[...], 0, 0)


def shift_kernel(spans, own_a, own_b, other_a, other_b, mods_ref, *refs):
    refs, outs = refs[:4], refs[4:]
    half = own_a.shape[0]
    added = mods_ref[2:3] * both_sums(0, 4 * half, *refs)
    own_added = jnp.concatenate([added[:half], added[2 * half : 3 * half]], axis=0)
    one_added = jnp.concatenate([added[half : 2 * half], added[3 * half :]], axis=0)
    own = jnp.concatenate([own_a[...], own_b[...]], axis=0).astype(jnp.float32) + own_added
    one = jnp.concatenate([other_a[:half], other_b[:half]], axis=0).astype(jnp.float32) + one_added
    for (first, last), straight_ref, crossing_ref in zip(spans, outs[::2], outs[1::2], strict=True):
        size = last - first
        straight_ref[:size] = own[first:last].astype(jnp.bfloat16)
        straight_ref[size:] = one[first:last].astype(jnp.bfloat16)
        crossing_ref[:size] = one_added[first:last].astype(jnp.bfloat16)
        crossing_ref[size:] = own_added[first:last].astype(jnp.bfloat16)


def shift(spans, owns, others, mods, mine, theirs, w_mine, w_theirs):
    rows, features, width = mine.shape[1], w_mine.shape[1], mine.shape[0]
    outs = [shape(jnp.bfloat16, 2 * (last - first), features) for first, last in spans for _ in range(2)]
    return call(
        functools.partial(shift_kernel, spans), outs, [],
        4 * rows * features * width, 0, (*owns, *others, mods, mine, theirs, w_mine, w_theirs),
    )


def join_kernel(straight_ref, crossing_ref, out_ref):
    total = straight_ref[...].astype(jnp.float32) + crossing_ref[...].astype(jnp.float32)
    out_ref[...] = total.astype(jnp.bfloat16)


def join(straight, crossing):
    return call(join_kernel, shape(straight.dtype, *straight.shape), [], straight.size, 0, (straight, crossing))


def part_kernel(first, *refs):
    *refs, out_ref = refs
    out_ref[...] = both_sums(first, first + out_ref.shape[0], *refs).astype(out_ref.dtype)


def part(first, dtype, mine, theirs, w_mine, w_theirs):
    rows, features, width = mine.shape[1] // 2, w_mine.shape[1], mine.shape[0]
    return call(
        functools.partial(part_kernel, first), shape(dtype, rows, features), [],
        4 * rows * features * width, 0, (mine, theirs, w_mine, w_theirs),
    )


def update_kernel(places, n_parts, mods_ref, *refs):
    parts, (mine_ref, theirs_ref, out_ref) = refs[:n_parts], refs[n_parts:]
    attended = mine_ref[...].astype(jnp.float32) + theirs_ref[...].astype(jnp.float32)
    at = 0
    for i, first, last in places:
        here = slice(at, at + last - first)
        new = parts[i][first:last].astype(jnp.float32) + mods_ref[2:3] * attended[here]
        out_ref[here] = new.astype(jnp.bfloat16)
        at += last - first


def update(parts, places, mods, mine, theirs):
    return call(
        functools.partial(update_kernel, places, len(parts)),
        shape(jnp.bfloat16, *mine.shape), [], 4 * mine.size, 0, (mods, *parts, mine, theirs),
    )


def halve_kernel(own_ref, a_ref, b_ref):
    half = a_ref.shape[0]
    a_ref[...] = own_ref[:half]
    b_ref[...] = own_ref[half:]


def halve(own):
    rows, features = own.shape
    return call(halve_kernel, [shape(own.dtype, rows // 2, features)] * 2, [], 0, 0, (own,))


def pack_kernel(first, own_ref, zero_ref, out_ref):
    half = own_ref.shape[0]
    out_ref[:half] = own_ref[...]
    out_ref[half:] = zero_ref[first : first + half]


def pack(own, first, zero):
    rows, features = own.shape
    return call(
        functools.partial(pack_kernel, first), shape(own.dtype, 2 * rows, features), [], 0, 0, (own, zero)
    )


def body(patches, qkv_weight, out_weight, modulation, stale_keys, stale_values, offsets):
    width = qkv_weight.shape[3]
    features = qkv_weight.shape[1]
    w = jnp.transpose(qkv_weight[0], (1, 2, 0)).reshape(3 * width, features)
    w_sent = out_weight[0]
    slots = offsets[0]
    own = patches[0]
    rows = own.shape[0]
    half = rows // 2
    spans = ((0, half), (half, rows))

    with jax.named_scope("first_gather"):
        zero = exchange(own, 0)
        owns = halve(own)
        packed = [pack(own_half, first, zero) for own_half, (first, _) in zip(owns, spans, strict=True)]
        others = [exchange(rows_here, 1) for rows_here in packed]
        w_sent, *_ = lax.optimization_barrier((w_sent, *packed))
        w_theirs = exchange(w_sent, 0)
    with jax.named_scope("prepare"):
        mods, w, w_mine, ko, vo, ko_next, vo_next = prepare(
            slots, modulation[0], w, out_weight[0], jnp.transpose(stale_keys[0]), jnp.transpose(stale_values[0])
        )
    with jax.named_scope("first_tick"):
        places = [((0, *span), (1, half, rows), (2, 0, half), (1, 0, half)) for span in spans]
        parts = [(zero, other, own_half) for other, own_half in zip(others, owns, strict=True)]
        mine, theirs, olds, _ = block(*parts, places, (), mods, w, ko, vo)
        cut = rows * SMALL_CHUNK // 16
        spans = ((0, cut), (cut, rows))
        shifted = shift(spans, owns, others, mods, mine, theirs, w_mine, w_theirs)
    with jax.named_scope("second_tick"):
        straights = [advance(straight, None) for straight in shifted[::2]]
        crossings = [advance(crossing, 1) for crossing in shifted[1::2]]
        here = [join(straight, crossing) for straight, crossing in zip(straights, crossings, strict=True)]
        others = [exchange(rows_here, 1) for rows_here in here]
        sizes = [last - first for first, last in spans]
        places = [(i, size, 2 * size) for i, size in enumerate(sizes)] + [(i, 0, size) for i, size in enumerate(sizes)]
        places = [tuple(places)] * 2
        mine, theirs, *_ = block(here, others, places, (slots, *olds), mods, w, ko_next, vo_next)
        from_one = exchange(part(rows, jnp.bfloat16, mine, theirs, w_mine, w_theirs), 1)
        mine_own = part(0, jnp.float32, mine, theirs, w_mine, w_theirs)
        own_rows = tuple((i, 0, size) for i, size in enumerate(sizes))
        return update(here, own_rows, mods, mine_own, from_one)[None]


def solution(mesh):
    placed = (
        P("pipe", "seq", None),
        P("pipe", None, None, "seq"),
        P("pipe", "seq", None),
        P("pipe", None, None),
        P("pipe", None, "seq"),
        P("pipe", None, "seq"),
        P("pipe", None),
    )
    return jax.shard_map(
        body, mesh=mesh, in_specs=placed, out_specs=P("pipe", "seq", None), check_vma=False
    )
```

```python
import functools
import math

import jax
import jax.numpy as jnp
from jax import lax
from jax.experimental import pallas as pl
from jax.experimental.pallas import tpu as pltpu
from jax.sharding import PartitionSpec as P

HEAD_DIM = 72
AXES = ("pipe", "seq")
SMALL_CHUNK = 6
VMEM_BYTES = 24 * 2**20
EXPONENT = math.log2(math.e) / math.sqrt(HEAD_DIM)


def partner(kind, section, member):
    if kind == 2:
        return member ^ 2
    if (kind + section) % 2 == 0:
        return member ^ 1
    return 3 - member


def exchange(array, kind):
    sections, members = lax.axis_size("pipe"), lax.axis_size("seq")
    moves = []
    for section in range(sections):
        for member in range(members):
            moves.append((section * members + partner(kind, section, member), section * members + member))
    return lax.ppermute(array, AXES, moves)


def advance(array, kind):
    sections, members = lax.axis_size("pipe"), lax.axis_size("seq")
    moves = []
    for section in range(sections):
        target = (section + 1) % sections
        for member in range(members):
            place = member if kind is None else partner(kind, section, member)
            moves.append((section * members + member, target * members + place))
    return lax.ppermute(array, AXES, moves)


def dot(a, b, contract_a, contract_b):
    return lax.dot_general(
        a, b, (((contract_a,), (contract_b,)), ((), ())), preferred_element_type=jnp.float32
    )


def normalize(rows, shift, scale):
    values = rows.astype(jnp.float32)
    center = jnp.mean(values, axis=-1, keepdims=True)
    values = values - center
    spread = jnp.mean(values * values, axis=-1, keepdims=True)
    return (values * lax.rsqrt(spread + 1e-06) * (1.0 + scale) + shift).astype(jnp.bfloat16)


def split_heads(source, refs):
    at = 0
    for ref in refs:
        for h in range(ref.shape[0]):
            ref[h] = source[at : at + HEAD_DIM].astype(jnp.bfloat16)
            at += HEAD_DIM


def attend(heads, jobs):
    scored = []
    for h in range(heads):
        for queries, caches, prior, store in jobs:
            q, pairs = queries(h), caches(h)
            scored.append((h, [dot(keys, q, 0, 0) for keys, _ in pairs], pairs, prior, store))
    for h, scores, pairs, prior, store in scored:
        top = functools.reduce(jnp.maximum, [jnp.max(s, 0, keepdims=True) for s in scores])
        total = out = 0.0
        if prior is not None:
            old_top, old_total, old_out = prior(h)
            top = jnp.maximum(top, old_top)
            shrink = jnp.exp2((old_top - top) * EXPONENT)
            total, out = old_total * shrink, old_out * shrink
        for s, (_, values) in zip(scores, pairs, strict=True):
            weights = jnp.exp2((s - top) * EXPONENT)
            total = total + jnp.sum(weights, 0, keepdims=True)
            out = out + dot(values, weights.astype(jnp.bfloat16), 1, 0)
        store(h, top, total, out)


def call(kernel, outs, scratch, flops, exps, operands, smem=()):
    specs = [pl.BlockSpec(memory_space=pltpu.SMEM if i in smem else pltpu.VMEM) for i in range(len(operands))]
    return pl.pallas_call(
        kernel,
        out_shape=outs,
        in_specs=specs,
        scratch_shapes=scratch,
        compiler_params=pltpu.CompilerParams(vmem_limit_bytes=VMEM_BYTES),
        cost_estimate=pl.CostEstimate(flops=flops, bytes_accessed=4 * 2**20, transcendentals=exps),
    )(*operands)


def shape(dtype, *sizes):
    return jax.ShapeDtypeStruct(sizes, dtype)


def prepare_kernel(offsets_ref, mods_ref, w_ref, wo_ref, stale_k_ref, stale_v_ref, mods_out, w_out, wo_out, *kept):
    mods_out[...] = mods_ref[...]
    w_out[...] = w_ref[...]
    wo_out[...] = wo_ref[...]
    count = kept[0].shape[2]
    for step in range(2):
        start = pl.multiple_of((1 - offsets_ref[step]) * count, count)
        for stale_ref, ref in zip((stale_k_ref, stale_v_ref), kept[2 * step : 2 * step + 2], strict=True):
            split_heads(stale_ref[:, pl.ds(start, count)].astype(jnp.float32), (ref,))


def prepare(offsets, mods, w, wo, stale_k, stale_v):
    width, context = stale_k.shape
    half = shape(jnp.bfloat16, width // HEAD_DIM, HEAD_DIM, context // 2)
    same = [shape(a.dtype, *a.shape) for a in (mods, w, wo)]
    return call(prepare_kernel, same + [half] * 4, [], 0, 0, (offsets, mods, w, wo, stale_k, stale_v), (0,))


def load_rows(refs, places, mods_ref, w_ref, normed, qkv):
    at = 0
    for i, first, last in places:
        normed[at : at + last - first] = normalize(refs[i][first:last], mods_ref[0:1], mods_ref[1:2])
        at += last - first
    qkv[...] = dot(w_ref[...], normed[...], 1, 1)


def early_kernel(places, n_parts, n_olds, *refs):
    parts, refs = refs[:n_parts], refs[n_parts:]
    olds, refs = refs[:n_olds], refs[n_olds:]
    mods_ref, w_ref, ko_ref, vo_ref, *outs, normed, qkv = refs
    q_ref, k_ref, v_ref, top_ref, total_ref, out_ref, *chosen = outs
    if olds:
        offsets_ref, *olds = olds
        for stale_ref, ref, old in zip((ko_ref, vo_ref), chosen, (olds[:2], olds[2:]), strict=True):
            ref[...] = stale_ref[...]

            @pl.when(offsets_ref[0] != offsets_ref[1])
            def _(ref=ref, old=old):
                split = old[0].shape[2]
                ref[:, :, :split] = old[0][...]
                ref[:, :, split:] = old[1][...]

        ko_ref, vo_ref = chosen
    load_rows(parts, places, mods_ref, w_ref, normed, qkv)
    split_heads(qkv, (q_ref, k_ref, v_ref))

    def store(h, top, total, out):
        top_ref[h : h + 1] = top
        total_ref[h : h + 1] = total
        out_ref[h] = out

    heads = q_ref.shape[0]
    attend(heads, [(lambda h: q_ref[h], lambda h: [(k_ref[h], v_ref[h]), (ko_ref[h], vo_ref[h])], None, store)])


def early(parts, places, olds, mods, w, ko, vo):
    rows, features = sum(last - first for _, first, last in places), w.shape[1]
    heads, _, count = ko.shape
    block = shape(jnp.bfloat16, heads, HEAD_DIM, rows)
    stat = shape(jnp.float32, 8, rows)
    chosen = [shape(jnp.bfloat16, *ko.shape)] * 2 if olds else []
    return call(
        functools.partial(early_kernel, places, len(parts), len(olds)),
        [block] * 3 + [stat, stat, shape(jnp.float32, heads, HEAD_DIM, rows)] + chosen,
        [pltpu.VMEM((rows, features), jnp.bfloat16), pltpu.VMEM((w.shape[0], rows), jnp.float32)],
        2 * rows * features * w.shape[0] + 4 * rows * (rows + count) * heads * HEAD_DIM,
        heads * rows * (rows + count), (*parts, *olds, mods, w, ko, vo), (len(parts),) if olds else (),
    )


def late_caches(late_refs, h):
    caches = late_refs[1:]
    return [(k_ref[h], v_ref[h]) for k_ref, v_ref in zip(caches[::2], caches[1::2], strict=True)]


def merge_job(mixed, at, span, early_refs, late_refs):
    q_ref, _, _, top_ref, total_ref, out_ref = early_refs
    first, last = span

    def store(h, top, total, out):
        mixed[h * HEAD_DIM : (h + 1) * HEAD_DIM, at : at + last - first] = out * (1.0 / total)

    return (
        lambda h: q_ref[h, :, first:last],
        lambda h: late_caches(late_refs, h),
        lambda h: (top_ref[h : h + 1, first:last], total_ref[h : h + 1, first:last], out_ref[h, :, first:last]),
        store,
    )


def whole_job(mixed, at, span, early_refs, late_refs, ko_ref, vo_ref):
    _, k_ref, v_ref, *_ = early_refs
    first, last = span

    def store(h, top, total, out):
        mixed[h * HEAD_DIM : (h + 1) * HEAD_DIM, at : at + last - first] = out * (1.0 / total)

    return (
        lambda h: late_refs[0][h, :, first:last],
        lambda h: [(k_ref[h], v_ref[h]), (ko_ref[h], vo_ref[h]), *late_caches(late_refs, h)],
        None,
        store,
    )


def finish(mixed, span, early_refs, late_refs, ko_ref, vo_ref):
    size = span[1] - span[0]
    attend(
        ko_ref.shape[0],
        [
            merge_job(mixed, 0, span, early_refs, late_refs),
            whole_job(mixed, size, span, early_refs, late_refs, ko_ref, vo_ref),
        ],
    )


def ahead_kernel(places, part_ref, mods_ref, w_ref, q_ref, k_ref, v_ref, normed, qkv):
    load_rows((part_ref,), places, mods_ref, w_ref, normed, qkv)
    split_heads(qkv, (q_ref, k_ref, v_ref))


def ahead(part, places, mods, w):
    rows, features = part.shape
    heads = w.shape[0] // HEAD_DIM // 3
    return call(
        functools.partial(ahead_kernel, places), [shape(jnp.bfloat16, heads, HEAD_DIM, rows)] * 3,
        [pltpu.VMEM((rows, features), jnp.bfloat16), pltpu.VMEM((w.shape[0], rows), jnp.float32)],
        2 * rows * features * w.shape[0], 0, (part, mods, w),
    )


def late_kernel(places, n_parts, n_ahead, *refs):
    parts, refs = refs[:n_parts], refs[n_parts:]
    before, refs = refs[:n_ahead], refs[n_ahead:]
    mods_ref, w_ref, ko_ref, vo_ref, *early_refs = refs[:10]
    sent_ref, *late_refs, normed, qkv, mixed = refs[10:]
    load_rows(parts, places, mods_ref, w_ref, normed, qkv)
    if before:
        q_ref, *late_refs = late_refs
        heads = q_ref.shape[0]
        new, old = qkv.shape[1] // 2, before[0].shape[2] // 2
        for h in range(heads):
            mine, theirs = qkv[h * HEAD_DIM : (h + 1) * HEAD_DIM], before[0][h].astype(jnp.float32)
            columns = [mine[:, :new], theirs[:, :old], mine[:, new:], theirs[:, old:]]
            q_ref[h] = jnp.concatenate(columns, axis=1).astype(jnp.bfloat16)
        split_heads(qkv[heads * HEAD_DIM :], late_refs)
        late_refs = (q_ref, *late_refs, *before[1:])
    else:
        split_heads(qkv, late_refs)
    finish(mixed, (0, mixed.shape[1] // 2), early_refs, late_refs, ko_ref, vo_ref)
    sent_ref[...] = mixed[...].astype(jnp.bfloat16)


def late(parts, places, mods, w, ko, vo, early_state, before=()):
    rows, features = sum(last - first for _, first, last in places), w.shape[1]
    heads, _, count = ko.shape
    width = heads * HEAD_DIM
    columns = rows + (before[0].shape[2] if before else 0)
    return call(
        functools.partial(late_kernel, places, len(parts), len(before)),
        [shape(jnp.bfloat16, width, columns), shape(jnp.bfloat16, heads, HEAD_DIM, columns)]
        + [shape(jnp.bfloat16, heads, HEAD_DIM, rows)] * 2,
        [
            pltpu.VMEM((rows, features), jnp.bfloat16),
            pltpu.VMEM((w.shape[0], rows), jnp.float32),
            pltpu.VMEM((width, columns), jnp.float32),
        ],
        2 * rows * features * w.shape[0] + 4 * columns * count * width,
        heads * columns * count, (*parts, *before, mods, w, ko, vo, *early_state),
    )


def rest_kernel(ko_ref, vo_ref, *refs):
    early_refs, (*late_refs, kept_ref, mixed) = refs[:6], refs[6:]
    columns = mixed.shape[1]
    finish(mixed, (columns // 2, columns), early_refs, late_refs, ko_ref, vo_ref)
    kept_ref[...] = mixed[...].astype(jnp.bfloat16)


def rest(ko, vo, early_state, late_state):
    heads, _, count = ko.shape
    width, rows = heads * HEAD_DIM, late_state[0].shape[2]
    return call(
        rest_kernel, shape(jnp.bfloat16, width, rows), [pltpu.VMEM((width, rows), jnp.float32)],
        64 * 4 * rows * count * width, heads * rows * count, (ko, vo, *early_state, *late_state),
    )


def block(early_parts, late_parts, places, olds, mods, w, ko, vo, first=None):
    state = early(early_parts, places[0], olds, mods, w, ko, vo)
    if olds:
        *state, ko, vo = state
    before = ahead(*first, mods, w) if first else ()
    sent, *late_state = late(late_parts, places[1], mods, w, ko, vo, state, before)
    theirs = exchange(sent, 0)
    mine = rest(ko, vo, state, (*late_state, *before[1:]))
    return mine, theirs, (state[1], late_state[1], state[2], late_state[2])


def both_sums(first, last, mine_ref, theirs_ref, w_mine_ref, w_theirs_ref):
    mine, theirs = (ref[:, first:last] for ref in (mine_ref, theirs_ref))
    return dot(mine, w_mine_ref[...], 0, 0) + dot(theirs, w_theirs_ref[...], 0, 0)


def shift_kernel(spans, own_a, own_b, other_a, other_b, mods_ref, *refs):
    refs, outs = refs[:4], refs[4:]
    half = own_a.shape[0]
    added = mods_ref[2:3] * both_sums(0, 4 * half, *refs)
    own_added = jnp.concatenate([added[:half], added[2 * half : 3 * half]], axis=0)
    one_added = jnp.concatenate([added[half : 2 * half], added[3 * half :]], axis=0)
    own = jnp.concatenate([own_a[...], own_b[...]], axis=0).astype(jnp.float32) + own_added
    one = jnp.concatenate([other_a[:half], other_b[:half]], axis=0).astype(jnp.float32) + one_added
    for (first, last), straight_ref, crossing_ref in zip(spans, outs[::2], outs[1::2], strict=True):
        size = last - first
        straight_ref[:size] = own[first:last].astype(jnp.bfloat16)
        straight_ref[size:] = one[first:last].astype(jnp.bfloat16)
        crossing_ref[:size] = one_added[first:last].astype(jnp.bfloat16)
        crossing_ref[size:] = own_added[first:last].astype(jnp.bfloat16)


def shift(spans, owns, others, mods, mine, theirs, w_mine, w_theirs):
    rows, features, width = mine.shape[1], w_mine.shape[1], mine.shape[0]
    outs = [shape(jnp.bfloat16, 2 * (last - first), features) for first, last in spans for _ in range(2)]
    return call(
        functools.partial(shift_kernel, spans), outs, [],
        4 * rows * features * width, 0, (*owns, *others, mods, mine, theirs, w_mine, w_theirs),
    )


def join_kernel(straight_ref, crossing_ref, out_ref):
    total = straight_ref[...].astype(jnp.float32) + crossing_ref[...].astype(jnp.float32)
    out_ref[...] = total.astype(jnp.bfloat16)


def join(straight, crossing):
    return call(join_kernel, shape(straight.dtype, *straight.shape), [], straight.size, 0, (straight, crossing))


def part_kernel(first, *refs):
    *refs, out_ref = refs
    out_ref[...] = both_sums(first, first + out_ref.shape[0], *refs).astype(out_ref.dtype)


def part(first, dtype, mine, theirs, w_mine, w_theirs):
    rows, features, width = mine.shape[1] // 2, w_mine.shape[1], mine.shape[0]
    return call(
        functools.partial(part_kernel, first), shape(dtype, rows, features), [],
        4 * rows * features * width, 0, (mine, theirs, w_mine, w_theirs),
    )


def update_kernel(places, n_parts, mods_ref, *refs):
    parts, (mine_ref, theirs_ref, out_ref) = refs[:n_parts], refs[n_parts:]
    attended = mine_ref[...].astype(jnp.float32) + theirs_ref[...].astype(jnp.float32)
    at = 0
    for i, first, last in places:
        here = slice(at, at + last - first)
        new = parts[i][first:last].astype(jnp.float32) + mods_ref[2:3] * attended[here]
        out_ref[here] = new.astype(jnp.bfloat16)
        at += last - first


def update(parts, places, mods, mine, theirs):
    return call(
        functools.partial(update_kernel, places, len(parts)),
        shape(jnp.bfloat16, *mine.shape), [], 4 * mine.size, 0, (mods, *parts, mine, theirs),
    )


def halve_kernel(own_ref, a_ref, b_ref):
    half = a_ref.shape[0]
    a_ref[...] = own_ref[:half]
    b_ref[...] = own_ref[half:]


def halve(own):
    rows, features = own.shape
    return call(halve_kernel, [shape(own.dtype, rows // 2, features)] * 2, [], 0, 0, (own,))


def pack_kernel(first, own_ref, zero_ref, out_ref):
    half = own_ref.shape[0]
    out_ref[:half] = own_ref[...]
    out_ref[half:] = zero_ref[first : first + half]


def pack(own, first, zero):
    rows, features = own.shape
    return call(
        functools.partial(pack_kernel, first), shape(own.dtype, 2 * rows, features), [], 0, 0, (own, zero)
    )


def body(patches, qkv_weight, out_weight, modulation, stale_keys, stale_values, offsets):
    width = qkv_weight.shape[3]
    features = qkv_weight.shape[1]
    w = jnp.transpose(qkv_weight[0], (1, 2, 0)).reshape(3 * width, features)
    w_sent = out_weight[0]
    slots = offsets[0]
    own = patches[0]
    rows = own.shape[0]
    half = rows // 2
    spans = ((0, half), (half, rows))

    with jax.named_scope("first_gather"):
        zero = exchange(own, 0)
        owns = halve(own)
        packed = [pack(own_half, first, zero) for own_half, (first, _) in zip(owns, spans, strict=True)]
        others = [exchange(rows_here, 1) for rows_here in packed]
        w_sent, *_ = lax.optimization_barrier((w_sent, *packed))
        w_theirs = exchange(w_sent, 0)
    with jax.named_scope("prepare"):
        mods, w, w_mine, ko, vo, ko_next, vo_next = prepare(
            slots, modulation[0], w, out_weight[0], jnp.transpose(stale_keys[0]), jnp.transpose(stale_values[0])
        )
    with jax.named_scope("first_tick"):
        places = [((0, *span), (1, half, rows), (2, 0, half), (1, 0, half)) for span in spans]
        parts = [(zero, other, own_half) for other, own_half in zip(others, owns, strict=True)]
        mine, theirs, olds = block(*parts, places, (), mods, w, ko, vo)
        cut = rows * SMALL_CHUNK // 16
        spans = ((0, cut), (cut, rows))
        shifted = shift(spans, owns, others, mods, mine, theirs, w_mine, w_theirs)
    with jax.named_scope("second_tick"):
        straights = [advance(straight, None) for straight in shifted[::2]]
        crossings = [advance(crossing, 1) for crossing in shifted[1::2]]
        here = [join(straight, crossing) for straight, crossing in zip(straights, crossings, strict=True)]
        others = [exchange(rows_here, 1) for rows_here in here]
        sizes = [last - first for first, last in spans]
        places = [(i, size, 2 * size) for i, size in enumerate(sizes)] + [(i, 0, size) for i, size in enumerate(sizes)]
        late_places = [((0, size, 2 * size), (0, 0, size)) for size in sizes]
        mine, theirs, _ = block(
            here, others[:1], (tuple(places), late_places[0]), (slots, *olds), mods, w, ko_next, vo_next,
            (others[1], late_places[1]),
        )
        from_one = exchange(part(rows, jnp.bfloat16, mine, theirs, w_mine, w_theirs), 1)
        mine_own = part(0, jnp.float32, mine, theirs, w_mine, w_theirs)
        own_rows = tuple((i, 0, size) for i, size in enumerate(sizes))
        return update(here, own_rows, mods, mine_own, from_one)[None]


def solution(mesh):
    placed = (
        P("pipe", "seq", None),
        P("pipe", None, None, "seq"),
        P("pipe", "seq", None),
        P("pipe", None, None),
        P("pipe", None, "seq"),
        P("pipe", None, "seq"),
        P("pipe", None),
    )
    return jax.shard_map(
        body, mesh=mesh, in_specs=placed, out_specs=P("pipe", "seq", None), check_vma=False
    )
```

```python
import functools
import math

import jax
import jax.numpy as jnp
from jax import lax
from jax.experimental import pallas as pl
from jax.experimental.pallas import tpu as pltpu
from jax.sharding import PartitionSpec as P

HEAD_DIM = 72
AXES = ("pipe", "seq")
SMALL_CHUNK = 6
VMEM_BYTES = 24 * 2**20
EXPONENT = math.log2(math.e) / math.sqrt(HEAD_DIM)


def partner(kind, section, member):
    if kind == 2:
        return member ^ 2
    if (kind + section) % 2 == 0:
        return member ^ 1
    return 3 - member


def exchange(array, kind):
    sections, members = lax.axis_size("pipe"), lax.axis_size("seq")
    moves = []
    for section in range(sections):
        for member in range(members):
            moves.append((section * members + partner(kind, section, member), section * members + member))
    return lax.ppermute(array, AXES, moves)


def advance(array, kind):
    sections, members = lax.axis_size("pipe"), lax.axis_size("seq")
    moves = []
    for section in range(sections):
        target = (section + 1) % sections
        for member in range(members):
            place = member if kind is None else partner(kind, section, member)
            moves.append((section * members + member, target * members + place))
    return lax.ppermute(array, AXES, moves)


def dot(a, b, contract_a, contract_b):
    return lax.dot_general(
        a, b, (((contract_a,), (contract_b,)), ((), ())), preferred_element_type=jnp.float32
    )


def normalize(rows, shift, scale):
    values = rows.astype(jnp.float32)
    center = jnp.mean(values, axis=-1, keepdims=True)
    values = values - center
    spread = jnp.mean(values * values, axis=-1, keepdims=True)
    return (values * lax.rsqrt(spread + 1e-06) * (1.0 + scale) + shift).astype(jnp.bfloat16)


def split_heads(source, refs):
    at = 0
    for ref in refs:
        for h in range(ref.shape[0]):
            ref[h] = source[at : at + HEAD_DIM].astype(jnp.bfloat16)
            at += HEAD_DIM


def attend(heads, jobs):
    scored = []
    for h in range(heads):
        for queries, caches, prior, store in jobs:
            q, pairs = queries(h), caches(h)
            scored.append((h, [dot(keys, q, 0, 0) for keys, _ in pairs], pairs, prior, store))
    for h, scores, pairs, prior, store in scored:
        top = functools.reduce(jnp.maximum, [jnp.max(s, 0, keepdims=True) for s in scores])
        total = out = 0.0
        if prior is not None:
            old_top, old_total, old_out = prior(h)
            top = jnp.maximum(top, old_top)
            shrink = jnp.exp2((old_top - top) * EXPONENT)
            total, out = old_total * shrink, old_out * shrink
        for s, (_, values) in zip(scores, pairs, strict=True):
            weights = jnp.exp2((s - top) * EXPONENT)
            total = total + jnp.sum(weights, 0, keepdims=True)
            out = out + dot(values, weights.astype(jnp.bfloat16), 1, 0)
        store(h, top, total, out)


def call(kernel, outs, scratch, flops, exps, operands, smem=()):
    specs = [pl.BlockSpec(memory_space=pltpu.SMEM if i in smem else pltpu.VMEM) for i in range(len(operands))]
    return pl.pallas_call(
        kernel,
        out_shape=outs,
        in_specs=specs,
        scratch_shapes=scratch,
        compiler_params=pltpu.CompilerParams(vmem_limit_bytes=VMEM_BYTES),
        cost_estimate=pl.CostEstimate(flops=flops, bytes_accessed=4 * 2**20, transcendentals=exps),
    )(*operands)


def shape(dtype, *sizes):
    return jax.ShapeDtypeStruct(sizes, dtype)


def prepare_kernel(offsets_ref, mods_ref, w_ref, wo_ref, stale_k_ref, stale_v_ref, mods_out, w_out, wo_out, *kept):
    mods_out[...] = mods_ref[...]
    w_out[...] = w_ref[...]
    wo_out[...] = wo_ref[...]
    count = kept[0].shape[2]
    for step in range(2):
        start = pl.multiple_of((1 - offsets_ref[step]) * count, count)
        for stale_ref, ref in zip((stale_k_ref, stale_v_ref), kept[2 * step : 2 * step + 2], strict=True):
            split_heads(stale_ref[:, pl.ds(start, count)].astype(jnp.float32), (ref,))


def prepare(offsets, mods, w, wo, stale_k, stale_v):
    width, context = stale_k.shape
    half = shape(jnp.bfloat16, width // HEAD_DIM, HEAD_DIM, context // 2)
    same = [shape(a.dtype, *a.shape) for a in (mods, w, wo)]
    return call(prepare_kernel, same + [half] * 4, [], 0, 0, (offsets, mods, w, wo, stale_k, stale_v), (0,))


def load_rows(refs, places, mods_ref, w_ref, normed, qkv):
    at = 0
    for i, first, last in places:
        normed[at : at + last - first] = normalize(refs[i][first:last], mods_ref[0:1], mods_ref[1:2])
        at += last - first
    qkv[...] = dot(w_ref[...], normed[...], 1, 1)


def early_kernel(places, n_parts, n_olds, *refs):
    parts, refs = refs[:n_parts], refs[n_parts:]
    olds, refs = refs[:n_olds], refs[n_olds:]
    mods_ref, w_ref, ko_ref, vo_ref, *outs, normed, qkv = refs
    q_ref, k_ref, v_ref, top_ref, total_ref, out_ref, *chosen = outs
    if olds:
        offsets_ref, *olds = olds
        for stale_ref, ref, old in zip((ko_ref, vo_ref), chosen, (olds[:2], olds[2:]), strict=True):
            ref[...] = stale_ref[...]

            @pl.when(offsets_ref[0] != offsets_ref[1])
            def _(ref=ref, old=old):
                split = old[0].shape[2]
                ref[:, :, :split] = old[0][...]
                ref[:, :, split:] = old[1][...]

        ko_ref, vo_ref = chosen
    load_rows(parts, places, mods_ref, w_ref, normed, qkv)
    split_heads(qkv, (q_ref, k_ref, v_ref))

    def store(h, top, total, out):
        top_ref[h : h + 1] = top
        total_ref[h : h + 1] = total
        out_ref[h] = out

    heads = q_ref.shape[0]
    attend(heads, [(lambda h: q_ref[h], lambda h: [(k_ref[h], v_ref[h]), (ko_ref[h], vo_ref[h])], None, store)])


def early(parts, places, olds, mods, w, ko, vo):
    rows, features = sum(last - first for _, first, last in places), w.shape[1]
    heads, _, count = ko.shape
    block = shape(jnp.bfloat16, heads, HEAD_DIM, rows)
    stat = shape(jnp.float32, 8, rows)
    chosen = [shape(jnp.bfloat16, *ko.shape)] * 2 if olds else []
    return call(
        functools.partial(early_kernel, places, len(parts), len(olds)),
        [block] * 3 + [stat, stat, shape(jnp.float32, heads, HEAD_DIM, rows)] + chosen,
        [pltpu.VMEM((rows, features), jnp.bfloat16), pltpu.VMEM((w.shape[0], rows), jnp.float32)],
        2 * rows * features * w.shape[0] + 4 * rows * (rows + count) * heads * HEAD_DIM,
        heads * rows * (rows + count), (*parts, *olds, mods, w, ko, vo), (len(parts),) if olds else (),
    )


def merge_job(mixed, at, span, early_refs, late_refs):
    q_ref, _, _, top_ref, total_ref, out_ref = early_refs
    _, kl_ref, vl_ref = late_refs
    first, last = span

    def store(h, top, total, out):
        mixed[h * HEAD_DIM : (h + 1) * HEAD_DIM, at : at + last - first] = out * (1.0 / total)

    return (
        lambda h: q_ref[h, :, first:last],
        lambda h: [(kl_ref[h], vl_ref[h])],
        lambda h: (top_ref[h : h + 1, first:last], total_ref[h : h + 1, first:last], out_ref[h, :, first:last]),
        store,
    )


def whole_job(mixed, at, span, early_refs, late_refs, ko_ref, vo_ref):
    _, k_ref, v_ref, *_ = early_refs
    ql_ref, kl_ref, vl_ref = late_refs
    first, last = span

    def store(h, top, total, out):
        mixed[h * HEAD_DIM : (h + 1) * HEAD_DIM, at : at + last - first] = out * (1.0 / total)

    return (
        lambda h: ql_ref[h, :, first:last],
        lambda h: [(k_ref[h], v_ref[h]), (ko_ref[h], vo_ref[h]), (kl_ref[h], vl_ref[h])],
        None,
        store,
    )


def finish(mixed, span, early_refs, late_refs, ko_ref, vo_ref):
    size = span[1] - span[0]
    attend(
        ko_ref.shape[0],
        [
            merge_job(mixed, 0, span, early_refs, late_refs),
            whole_job(mixed, size, span, early_refs, late_refs, ko_ref, vo_ref),
        ],
    )


def late_kernel(places, n_parts, *refs):
    parts, refs = refs[:n_parts], refs[n_parts:]
    mods_ref, w_ref, ko_ref, vo_ref, *early_refs = refs[:10]
    sent_ref, *late_refs, normed, qkv, mixed = refs[10:]
    load_rows(parts, places, mods_ref, w_ref, normed, qkv)
    split_heads(qkv, late_refs)
    finish(mixed, (0, mixed.shape[1] // 2), early_refs, late_refs, ko_ref, vo_ref)
    sent_ref[...] = mixed[...].astype(jnp.bfloat16)


def late(parts, places, mods, w, ko, vo, early_state):
    rows, features = sum(last - first for _, first, last in places), w.shape[1]
    heads, _, count = ko.shape
    width = heads * HEAD_DIM
    return call(
        functools.partial(late_kernel, places, len(parts)),
        [shape(jnp.bfloat16, width, rows)] + [shape(jnp.bfloat16, heads, HEAD_DIM, rows)] * 3,
        [
            pltpu.VMEM((rows, features), jnp.bfloat16),
            pltpu.VMEM((w.shape[0], rows), jnp.float32),
            pltpu.VMEM((width, rows), jnp.float32),
        ],
        2 * rows * features * w.shape[0] + 4 * rows * count * width,
        heads * rows * count, (*parts, mods, w, ko, vo, *early_state),
    )


def rest_kernel(ko_ref, vo_ref, *refs):
    early_refs, late_refs, (kept_ref, mixed) = refs[:6], refs[6:9], refs[9:]
    columns = mixed.shape[1]
    finish(mixed, (columns // 2, columns), early_refs, late_refs, ko_ref, vo_ref)
    kept_ref[...] = mixed[...].astype(jnp.bfloat16)


def rest(ko, vo, early_state, late_state):
    heads, _, count = ko.shape
    width, rows = heads * HEAD_DIM, late_state[0].shape[2]
    return call(
        rest_kernel, shape(jnp.bfloat16, width, rows), [pltpu.VMEM((width, rows), jnp.float32)],
        64 * 4 * rows * count * width, heads * rows * count, (ko, vo, *early_state, *late_state),
    )


def block(early_parts, late_parts, places, olds, mods, w, ko, vo, also=()):
    state = early(early_parts, places[0], olds, mods, w, ko, vo)
    if olds:
        *state, ko, vo = state
    sent, *late_state = late(late_parts, places[1], mods, w, ko, vo, state)
    theirs = exchange(sent, 0)
    mine = rest(ko, vo, state, late_state)
    return mine, theirs, (state[1], late_state[1], state[2], late_state[2]), also


def both_sums(first, last, mine_ref, theirs_ref, w_mine_ref, w_theirs_ref):
    mine, theirs = (ref[:, first:last] for ref in (mine_ref, theirs_ref))
    return dot(mine, w_mine_ref[...], 0, 0) + dot(theirs, w_theirs_ref[...], 0, 0)


def shift_kernel(spans, own_a, own_b, other_a, other_b, mods_ref, *refs):
    refs, outs = refs[:4], refs[4:]
    half = own_a.shape[0]
    added = mods_ref[2:3] * both_sums(0, 4 * half, *refs)
    own_added = jnp.concatenate([added[:half], added[2 * half : 3 * half]], axis=0)
    one_added = jnp.concatenate([added[half : 2 * half], added[3 * half :]], axis=0)
    own = jnp.concatenate([own_a[...], own_b[...]], axis=0).astype(jnp.float32) + own_added
    one = jnp.concatenate([other_a[:half], other_b[:half]], axis=0).astype(jnp.float32) + one_added
    for (first, last), straight_ref, crossing_ref in zip(spans, outs[::2], outs[1::2], strict=True):
        size = last - first
        straight_ref[:size] = own[first:last].astype(jnp.bfloat16)
        straight_ref[size:] = one[first:last].astype(jnp.bfloat16)
        crossing_ref[:size] = one_added[first:last].astype(jnp.bfloat16)
        crossing_ref[size:] = own_added[first:last].astype(jnp.bfloat16)


def shift(spans, owns, others, mods, mine, theirs, w_mine, w_theirs):
    rows, features, width = mine.shape[1], w_mine.shape[1], mine.shape[0]
    outs = [shape(jnp.bfloat16, 2 * (last - first), features) for first, last in spans for _ in range(2)]
    return call(
        functools.partial(shift_kernel, spans), outs, [],
        4 * rows * features * width, 0, (*owns, *others, mods, mine, theirs, w_mine, w_theirs),
    )


def join_kernel(straight_ref, crossing_ref, out_ref):
    total = straight_ref[...].astype(jnp.float32) + crossing_ref[...].astype(jnp.float32)
    out_ref[...] = total.astype(jnp.bfloat16)


def join(straight, crossing):
    return call(join_kernel, shape(straight.dtype, *straight.shape), [], straight.size, 0, (straight, crossing))


def part_kernel(first, *refs):
    *refs, out_ref = refs
    out_ref[...] = both_sums(first, first + out_ref.shape[0], *refs).astype(out_ref.dtype)


def part(first, dtype, mine, theirs, w_mine, w_theirs):
    rows, features, width = mine.shape[1] // 2, w_mine.shape[1], mine.shape[0]
    return call(
        functools.partial(part_kernel, first), shape(dtype, rows, features), [],
        4 * rows * features * width, 0, (mine, theirs, w_mine, w_theirs),
    )


def base_kernel(places, n_parts, mods_ref, *refs):
    parts, (*refs, out_ref) = refs[:n_parts], refs[n_parts:]
    added = mods_ref[2:3] * both_sums(0, out_ref.shape[0], *refs)
    at = 0
    for i, first, last in places:
        here = slice(at, at + last - first)
        out_ref[here] = parts[i][first:last].astype(jnp.float32) + added[here]
        at += last - first


def base(parts, places, mods, mine, theirs, w_mine, w_theirs):
    rows, features, width = mine.shape[1] // 2, w_mine.shape[1], mine.shape[0]
    return call(
        functools.partial(base_kernel, places, len(parts)), shape(jnp.float32, rows, features), [],
        4 * rows * features * width, 0, (mods, *parts, mine, theirs, w_mine, w_theirs),
    )


def update_kernel(base_ref, mods_ref, theirs_ref, out_ref):
    out_ref[...] = (base_ref[...] + mods_ref[2:3] * theirs_ref[...].astype(jnp.float32)).astype(jnp.bfloat16)


def update(hidden, mods, theirs):
    return call(update_kernel, shape(jnp.bfloat16, *hidden.shape), [], 2 * hidden.size, 0, (hidden, mods, theirs))


def halve_kernel(own_ref, a_ref, b_ref):
    half = a_ref.shape[0]
    a_ref[...] = own_ref[:half]
    b_ref[...] = own_ref[half:]


def halve(own):
    rows, features = own.shape
    return call(halve_kernel, [shape(own.dtype, rows // 2, features)] * 2, [], 0, 0, (own,))


def pack_kernel(first, own_ref, zero_ref, out_ref):
    half = own_ref.shape[0]
    out_ref[:half] = own_ref[...]
    out_ref[half:] = zero_ref[first : first + half]


def pack(own, first, zero):
    rows, features = own.shape
    return call(
        functools.partial(pack_kernel, first), shape(own.dtype, 2 * rows, features), [], 0, 0, (own, zero)
    )


def body(patches, qkv_weight, out_weight, modulation, stale_keys, stale_values, offsets):
    width = qkv_weight.shape[3]
    features = qkv_weight.shape[1]
    w = jnp.transpose(qkv_weight[0], (1, 2, 0)).reshape(3 * width, features)
    w_sent = out_weight[0]
    slots = offsets[0]
    own = patches[0]
    rows = own.shape[0]
    half = rows // 2
    spans = ((0, half), (half, rows))

    with jax.named_scope("first_gather"):
        zero = exchange(own, 0)
        owns = halve(own)
        packed = [pack(own_half, first, zero) for own_half, (first, _) in zip(owns, spans, strict=True)]
        others = [exchange(rows_here, 1) for rows_here in packed]
        w_sent, *_ = lax.optimization_barrier((w_sent, *packed))
        w_theirs = exchange(w_sent, 0)
    with jax.named_scope("prepare"):
        mods, w, w_mine, ko, vo, ko_next, vo_next = prepare(
            slots, modulation[0], w, out_weight[0], jnp.transpose(stale_keys[0]), jnp.transpose(stale_values[0])
        )
    with jax.named_scope("first_tick"):
        places = [((0, *span), (1, half, rows), (2, 0, half), (1, 0, half)) for span in spans]
        parts = [(zero, other, own_half) for other, own_half in zip(others, owns, strict=True)]
        mine, theirs, olds, _ = block(*parts, places, (), mods, w, ko, vo)
        cut = rows * SMALL_CHUNK // 16
        spans = ((0, cut), (cut, rows))
        shifted = shift(spans, owns, others, mods, mine, theirs, w_mine, w_theirs)
    with jax.named_scope("second_tick"):
        straights = [advance(straight, None) for straight in shifted[::2]]
        crossings = [advance(crossing, 1) for crossing in shifted[1::2]]
        here = [join(straight, crossing) for straight, crossing in zip(straights, crossings, strict=True)]
        others = [exchange(rows_here, 1) for rows_here in here]
        sizes = [last - first for first, last in spans]
        places = [(i, size, 2 * size) for i, size in enumerate(sizes)] + [(i, 0, size) for i, size in enumerate(sizes)]
        places = [tuple(places)] * 2
        mine, theirs, *_ = block(here, others, places, (slots, *olds), mods, w, ko_next, vo_next)
        from_one = exchange(part(rows, jnp.bfloat16, mine, theirs, w_mine, w_theirs), 1)
        own_rows = tuple((i, 0, size) for i, size in enumerate(sizes))
        return update(base(here, own_rows, mods, mine, theirs, w_mine, w_theirs), mods, from_one)[None]


def solution(mesh):
    placed = (
        P("pipe", "seq", None),
        P("pipe", None, None, "seq"),
        P("pipe", "seq", None),
        P("pipe", None, None),
        P("pipe", None, "seq"),
        P("pipe", None, "seq"),
        P("pipe", None),
    )
    return jax.shard_map(
        body, mesh=mesh, in_specs=placed, out_specs=P("pipe", "seq", None), check_vma=False
    )
```
